32 devices in a mesh: curve: 8 (over z, x), group: 4 (over y, core).
Axes of the slice: x: 2, y: 2, z: 4, core: 2. Of those that a mesh axis runs over, the one named last changes fastest.
Arguments:
- right_side: float32 [64, 8192], P(None, ('curve', 'group')), may hold values from -6 to 6
- start_field: float32 [64, 8192], P(None, ('curve', 'group')), may hold values from -3 to 3
- block_level: int32 [8192], P(('curve', 'group')), may hold values from 0 to 3
- neighbors: int32 [8, 8192], P(None, ('curve', 'group')), may hold values from -64 to 64, as said below
- neighbor_kinds: int32 [8, 8192], P(None, ('curve', 'group')), may hold values from 0 to 29
- owners_zero: int32 [2, 8192], P(None, ('curve', 'group')), may hold values from 0 to 63, as said below
- owners_one: int32 [2, 2048], P(None, 'curve'), may hold values from 0 to 63, as said below
- owners_two: int32 [2, 512], P(None, 'curve'), may hold values from 0 to 15, as said below
- owners_three: int32 [2, 128], replicated, may hold values from 0 to 7, as said below
- coarse_neighbors: int32 [8, 32], replicated, may hold values from -1 to 31, as said below
- coarse_kinds: int32 [8, 32], replicated, may hold values from 0 to 29
- coarse_level: int32 [32], replicated, may hold values from 0 to 3
- stiffness: float32 [64, 64], replicated
- smoother: float32 [64, 64], replicated
- couplings: float32 [30, 64, 64], replicated, may hold values from -0.18 to 0.18
- restriction: float32 [8, 64, 64], replicated, may hold values from -0.375 to 0.375
Outputs:
- smoothed: float32 [64, 8192], P(None, ('curve', 'group'))
The draws below stay inside these ranges and needn't reach their ends.
Inputs may be any that keep to these rules, and one draw needn't show every extreme that they name: `neighbors`: 0 where a slot couples to nothing, else the nonzero offset to another fine block inside the grid; in slot 0 the first block of each device's range has offset exactly -64 and the last exactly 64 wherever that neighbour exists. `owners_zero`: row 0: within each device's 256 blocks, slots of 64 level-one blocks that never fall, every slot used by 1 to 8 blocks and by 8 in some; row 1: octant. `owners_one`: row 0: within each curve index's level-one blocks, slots of 64 level-two blocks that never fall, every slot used by 1 to 8 blocks and by 8 in some; row 1: octant. `owners_two`: row 0: within each curve index's 64 blocks, slots of 16 level-three blocks that never fall, every slot used by 1 to 8 blocks and by 8 in some; row 1: octant. `owners_three`: row 0: within each curve index's 16 blocks, slots of 4 level-four blocks that never fall, every slot used by 1 to 8 blocks and by 8 in some; row 1: octant. `coarse_neighbors`: -1 where a slot couples to nothing, else another level-four block.
All inputs are finite; a program needn't handle non-finite values.
Results may differ from the reference program's by a relative error of at most 0.0003.
Values sent between devices are 32-bit elements; how exact they have to be, the bound alone decides.
A program may use at most 64 MiB of HBM per device.

```python
import jax
import jax.numpy as jnp
from jax import lax

VALUES = 64
BLOCK_DEV = 256
FACE_SLOTS = 8
MORTAR_KINDS = 30
OCTANTS = 8
HALO_SPAN = 64
PRE_SWEEPS = 2
COARSE_SWEEPS = 3
LEVEL_ONE = 64
LEVEL_TWO = 64
LEVEL_THREE = 16
LEVEL_FOUR = 4
FINE_BLOCKS = 8192
BLOCKS_ONE = 2048
BLOCKS_TWO = 512
BLOCKS_THREE = 128
BLOCKS_FOUR = 32
N_CURVE = 8
N_GROUP = 4


def family_lists(key, row_count, row_length):
    parent_count = row_length // 4
    key_pair, key_first, key_second, key_octant = jax.random.split(key, 4)
    paired = jax.random.randint(key_pair, (row_count, parent_count // 2), 1, 8)
    sizes = jnp.stack([paired, 8 - paired], axis=-1).reshape(row_count, parent_count)
    first_size = jax.random.randint(key_first, (row_count,), 1, 7)
    second_size = 1 + jax.random.randint(key_second, (row_count,), 0, 7 - first_size)
    third_size = 8 - first_size - second_size
    head_sizes = jnp.stack([jnp.full((row_count,), 8, jnp.int32), first_size, second_size, third_size], axis=-1)
    sizes = jnp.concatenate([head_sizes.astype(jnp.int32), sizes[:, 4:].astype(jnp.int32)], axis=1)
    ends = jnp.cumsum(sizes, axis=1)
    positions = jnp.arange(row_length, dtype=jnp.int32)
    parent = jnp.sum((ends[:, :, None] <= positions[None, None, :]).astype(jnp.int32), axis=1)
    octant = jax.random.randint(key_octant, (row_count, row_length), 0, 8)
    return jnp.stack([parent.reshape(-1), octant.reshape(-1)]).astype(jnp.int32)


def draw_owners_zero(key, part):
    return family_lists(jax.random.fold_in(key, 11), FINE_BLOCKS // BLOCK_DEV, BLOCK_DEV)


def draw_owners_one(key, part):
    return family_lists(jax.random.fold_in(key, 12), BLOCKS_ONE // (4 * LEVEL_TWO), 4 * LEVEL_TWO)


def draw_owners_two(key, part):
    return family_lists(jax.random.fold_in(key, 13), BLOCKS_TWO // LEVEL_TWO, LEVEL_TWO)


def draw_owners_three(key, part):
    return family_lists(jax.random.fold_in(key, 14), BLOCKS_THREE // LEVEL_THREE, LEVEL_THREE)


def draw_neighbors(key, part):
    key_step, key_sign, key_keep = jax.random.split(jax.random.fold_in(key, 21), 3)
    blocks = jnp.arange(FINE_BLOCKS, dtype=jnp.int32)[None, :]
    step_size = jax.random.randint(key_step, (FACE_SLOTS, FINE_BLOCKS), 1, HALO_SPAN + 1)
    direction = 2 * jax.random.randint(key_sign, (FACE_SLOTS, FINE_BLOCKS), 0, 2) - 1
    offset = direction * step_size
    keep_slot = jax.random.randint(key_keep, (FACE_SLOTS, FINE_BLOCKS), 0, 4) > 0
    slot_ids = jnp.arange(FACE_SLOTS, dtype=jnp.int32)[:, None]
    within = blocks % BLOCK_DEV
    force_back = (slot_ids == 0) & (within == 0)
    force_ahead = (slot_ids == 0) & (within == BLOCK_DEV - 1)
    offset = jnp.where(force_back, -HALO_SPAN, jnp.where(force_ahead, HALO_SPAN, offset))
    keep_slot = keep_slot | force_back | force_ahead
    target = blocks + offset
    inside = (target >= 0) & (target < FINE_BLOCKS)
    return jnp.where(keep_slot & inside, offset, 0).astype(jnp.int32)


def draw_coarse_neighbors(key, part):
    key_target, key_keep = jax.random.split(jax.random.fold_in(key, 31), 2)
    blocks = jnp.arange(BLOCKS_FOUR, dtype=jnp.int32)[None, :]
    target = jax.random.randint(key_target, (FACE_SLOTS, BLOCKS_FOUR), 0, BLOCKS_FOUR - 1)
    target = jnp.where(target >= blocks, target + 1, target)
    keep_slot = jax.random.randint(key_keep, (FACE_SLOTS, BLOCKS_FOUR), 0, 4) > 0
    return jnp.where(keep_slot, target, -1).astype(jnp.int32)


def draw_stiffness(key, part):
    inner_key = jax.random.fold_in(key, 41)
    spread = 0.05 * jax.random.normal(inner_key, (VALUES, VALUES), jnp.float32)
    return 2.0 * jnp.eye(VALUES, dtype=jnp.float32) + spread


def draw_smoother(key, part):
    inner_key = jax.random.fold_in(key, 42)
    spread = 0.0125 * jax.random.normal(inner_key, (VALUES, VALUES), jnp.float32)
    return 0.5 * jnp.eye(VALUES, dtype=jnp.float32) + spread


def set_ends(drawn, key, smallest, top_value):
    longest = drawn.shape.index(max(drawn.shape))
    spots = []
    for shift in (0, 1):
        where = [jax.random.randint(jax.random.fold_in(key, axis), (), 0, length) for axis, length in enumerate(drawn.shape)]
        where[longest] = (where[longest] + shift) % drawn.shape[longest]
        spots.append(tuple(where))
    return drawn.at[spots[0]].set(smallest).at[spots[1]].set(top_value)


def block_levels(own_key, dims, cuts, least, largest):
    def one(axis_at, blocks):
        heights = jax.random.uniform(jax.random.fold_in(jax.random.fold_in(own_key, 6), axis_at), (blocks,), jnp.float32, least / len(cuts), largest / len(cuts))
        return jnp.repeat(jnp.exp(heights), dims[axis_at] // blocks).reshape((-1,) + (1,) * (len(dims) - axis_at - 1))

    factor_of = one(*cuts[0])
    for cut in cuts[1:]:
        factor_of = factor_of * one(*cut)
    return factor_of


def noise(stream_key, shape, scale, bound, cuts=(), held_as=jnp.bfloat16):
    array = scale * jax.random.normal(stream_key, shape, jnp.float32)
    if cuts:
        array = array * block_levels(stream_key, shape, cuts, -0.22, 0.18)
    return jnp.clip(array, -bound, bound).astype(held_as)


def setup_inputs(seed: int = 0) -> dict:
    streams_of = jax.random.split(jax.random.key(seed), 17)
    right_side = noise(streams_of[0], (VALUES, FINE_BLOCKS), 1.0, 6.0, ((1, 32),), jnp.float32)
    start_field = noise(streams_of[1], (VALUES, FINE_BLOCKS), 0.5, 3.0, ((1, 32),), jnp.float32)
    block_level = set_ends(jax.random.randint(streams_of[2], (FINE_BLOCKS,), 0, 4), jax.random.fold_in(streams_of[2], 1), 0, 3).astype(jnp.int32)
    neighbors = draw_neighbors(jax.random.fold_in(streams_of[16], 71), 0)
    neighbor_kinds = set_ends(jax.random.randint(streams_of[4], (FACE_SLOTS, FINE_BLOCKS), 0, MORTAR_KINDS), jax.random.fold_in(streams_of[4], 1), 0, MORTAR_KINDS - 1).astype(jnp.int32)
    owners_zero = draw_owners_zero(jax.random.fold_in(streams_of[16], 71), 0)
    owners_one = draw_owners_one(jax.random.fold_in(streams_of[16], 71), 0)
    owners_two = draw_owners_two(jax.random.fold_in(streams_of[16], 71), 0)
    owners_three = draw_owners_three(jax.random.fold_in(streams_of[16], 71), 0)
    coarse_neighbors = draw_coarse_neighbors(jax.random.fold_in(streams_of[16], 71), 0)
    coarse_kinds = set_ends(jax.random.randint(streams_of[10], (FACE_SLOTS, BLOCKS_FOUR), 0, MORTAR_KINDS), jax.random.fold_in(streams_of[10], 1), 0, MORTAR_KINDS - 1).astype(jnp.int32)
    coarse_level = set_ends(jax.random.randint(streams_of[11], (BLOCKS_FOUR,), 0, 4), jax.random.fold_in(streams_of[11], 1), 0, 3).astype(jnp.int32)
    stiffness = draw_stiffness(jax.random.fold_in(streams_of[16], 71), 0)
    smoother = draw_smoother(jax.random.fold_in(streams_of[16], 71), 0)
    couplings = noise(streams_of[14], (MORTAR_KINDS, VALUES, VALUES), 0.03, 0.18, (), jnp.float32)
    restriction = noise(streams_of[15], (OCTANTS, VALUES, VALUES), 256 ** -0.5, 0.375, (), jnp.float32)
    return {"right_side": right_side, "start_field": start_field, "block_level": block_level, "neighbors": neighbors, "neighbor_kinds": neighbor_kinds, "owners_zero": owners_zero, "owners_one": owners_one, "owners_two": owners_two, "owners_three": owners_three, "coarse_neighbors": coarse_neighbors, "coarse_kinds": coarse_kinds, "coarse_level": coarse_level, "stiffness": stiffness, "smoother": smoother, "couplings": couplings, "restriction": restriction}


DAMPING = 0.7
PRECISE = lax.Precision.HIGHEST


def couple_sum(values, neighbor_index, kinds, couplings):
    is_valid = neighbor_index >= 0
    safe_index = jnp.where(is_valid, neighbor_index, 0)
    picked = jnp.take(values, safe_index.reshape(-1), axis=1)
    picked = picked.reshape(values.shape[0], neighbor_index.shape[0], neighbor_index.shape[1])
    picked = picked * is_valid[None].astype(jnp.float32)
    kind_ids = lax.broadcasted_iota(jnp.int32, (couplings.shape[0], 1, 1), 0)
    onehot = (kinds[None] == kind_ids).astype(jnp.float32)
    grouped = jnp.einsum("tkm,pkm->tpm", onehot, picked, precision=PRECISE)
    return jnp.einsum("tqp,tpm->qm", couplings, grouped, precision=PRECISE)


def apply_block(window, own_values, neighbor_index, kinds, scales, stiffness, couplings):
    inner_sum = jnp.dot(stiffness, own_values, precision=PRECISE) + couple_sum(window, neighbor_index, kinds, couplings)
    return scales[None, :] * inner_sum


def smooth_step(iterate, applied, rhs_values, scales, smoother):
    return iterate + DAMPING * jnp.dot(smoother, (rhs_values - applied) / scales[None, :], precision=PRECISE)


def octant_masks(octant, matrices):
    octant_ids = lax.broadcasted_iota(jnp.int32, (matrices.shape[0], 1, 1), 0)
    return (octant[None, None, :] == octant_ids).astype(jnp.float32)


def restrict(values, owners, parent_count, matrices):
    oct_masks = octant_masks(owners[1], matrices)
    mapped = jnp.einsum("oqp,opn->qn", matrices, values[None] * oct_masks, precision=PRECISE)
    slot_ids = lax.broadcasted_iota(jnp.int32, (1, parent_count), 1)
    onehot = (owners[0][:, None] == slot_ids).astype(jnp.float32)
    return jnp.dot(mapped, onehot, precision=PRECISE)


def prolong(values, owners, matrices):
    oct_masks = octant_masks(owners[1], matrices)
    slot_ids = lax.broadcasted_iota(jnp.int32, (1, values.shape[1]), 1)
    onehot = (owners[0][:, None] == slot_ids).astype(jnp.float32)
    pulled = jnp.dot(values, onehot.T, precision=PRECISE)
    mapped = jnp.einsum("oqp,qn->opn", matrices, pulled, precision=PRECISE)
    return jnp.sum(mapped * oct_masks, axis=0)


def grouped_restrict(values, owners, groups, parent_count, matrices):
    group_width = values.shape[1] // groups

    def per_group(group_index):
        first_col = group_index * group_width
        columns = lax.dynamic_slice_in_dim(values, first_col, group_width, 1)
        own_owners = lax.dynamic_slice_in_dim(owners, first_col, group_width, 1)
        return restrict(columns, own_owners, parent_count, matrices)

    pieces = lax.map(per_group, jnp.arange(groups, dtype=jnp.int32))
    return jnp.transpose(pieces, (1, 0, 2)).reshape(values.shape[0], groups * parent_count)


def grouped_prolong(values, owners, groups, matrices):
    parent_width = values.shape[1] // groups
    child_width = owners.shape[1] // groups

    def per_group(group_index):
        columns = lax.dynamic_slice_in_dim(values, group_index * parent_width, parent_width, 1)
        own_owners = lax.dynamic_slice_in_dim(owners, group_index * child_width, child_width, 1)
        return prolong(columns, own_owners, matrices)

    pieces = lax.map(per_group, jnp.arange(groups, dtype=jnp.int32))
    return jnp.transpose(pieces, (1, 0, 2)).reshape(values.shape[0], groups * child_width)


def fine_image(iterate, neighbors, kinds, scales, stiffness, couplings):
    padded = jnp.pad(iterate, ((0, 0), (HALO_SPAN, HALO_SPAN)))
    local_ids = jnp.arange(BLOCK_DEV, dtype=jnp.int32)[None, :]

    def per_device(device_index):
        first_block = (device_index * BLOCK_DEV).astype(jnp.int32)
        window = lax.dynamic_slice_in_dim(padded, first_block, BLOCK_DEV + 2 * HALO_SPAN, 1)
        own_values = lax.dynamic_slice_in_dim(iterate, first_block, BLOCK_DEV, 1)
        own_offset = lax.dynamic_slice_in_dim(neighbors, first_block, BLOCK_DEV, 1)
        own_kinds = lax.dynamic_slice_in_dim(kinds, first_block, BLOCK_DEV, 1)
        own_scales = lax.dynamic_slice_in_dim(scales, first_block, BLOCK_DEV, 0)
        window_index = jnp.where(own_offset != 0, local_ids + own_offset + HALO_SPAN, -1).astype(jnp.int32)
        return apply_block(window, own_values, window_index, own_kinds, own_scales, stiffness, couplings)

    pieces = lax.map(per_device, jnp.arange(N_CURVE * N_GROUP, dtype=jnp.int32))
    return jnp.transpose(pieces, (1, 0, 2)).reshape(iterate.shape[0], FINE_BLOCKS)


def reference(right_side, start_field, block_level, neighbors, neighbor_kinds, owners_zero, owners_one, owners_two, owners_three, coarse_neighbors, coarse_kinds, coarse_level, stiffness, smoother, couplings, restriction):
    scales = jnp.exp2(-block_level.astype(jnp.float32))
    iterate = start_field
    for sweep_index in range(PRE_SWEEPS):
        applied = fine_image(iterate, neighbors, neighbor_kinds, scales, stiffness, couplings)
        iterate = smooth_step(iterate, applied, right_side, scales, smoother)
    residual = right_side - fine_image(iterate, neighbors, neighbor_kinds, scales, stiffness, couplings)
    level_one = grouped_restrict(residual, owners_zero, N_CURVE * N_GROUP, LEVEL_ONE, restriction)
    level_two = grouped_restrict(level_one, owners_one, N_CURVE, LEVEL_TWO, restriction)
    level_three = grouped_restrict(level_two, owners_two, N_CURVE, LEVEL_THREE, restriction)
    coarse_rhs = grouped_restrict(level_three, owners_three, N_CURVE, LEVEL_FOUR, restriction)
    coarse_scales = jnp.exp2(-coarse_level.astype(jnp.float32))
    zero_field = jnp.zeros_like(coarse_rhs)
    correction = smooth_step(zero_field, zero_field, coarse_rhs, coarse_scales, smoother)
    for sweep_index in range(COARSE_SWEEPS - 1):
        applied = apply_block(correction, correction, coarse_neighbors, coarse_kinds, coarse_scales, stiffness, couplings)
        correction = smooth_step(correction, applied, coarse_rhs, coarse_scales, smoother)
    back_three = grouped_prolong(correction, owners_three, N_CURVE, restriction)
    back_two = grouped_prolong(back_three, owners_two, N_CURVE, restriction)
    back_one = grouped_prolong(back_two, owners_one, N_CURVE, restriction)
    back_zero = grouped_prolong(back_one, owners_zero, N_CURVE * N_GROUP, restriction)
    iterate = iterate + back_zero
    applied = fine_image(iterate, neighbors, neighbor_kinds, scales, stiffness, couplings)
    return smooth_step(iterate, applied, right_side, scales, smoother)
```

```python
import functools

import jax
import jax.numpy as jnp
from jax import lax
from jax.experimental import pallas as pl
from jax.experimental.pallas import tpu as pltpu
from jax.sharding import PartitionSpec as P

DAMPING = 0.7
COARSE_SWEEPS = 3
LANES = 128
HALF = 64
F32, BF16 = jnp.float32, jnp.bfloat16
MESH = pl.DeviceIdType.MESH


def split(x):
    hi = x.astype(BF16)
    return hi, (x - hi.astype(F32)).astype(BF16)


def stack(x):
    return jnp.concatenate(split(x), axis=0)


def side(x):
    return jnp.concatenate(split(x), axis=1)


def fold(r):
    n = r.shape[0] // 2
    return (r[:n, :LANES] + r[n:, :LANES]) + r[:n, LANES:]


def times(left, x):
    return fold(jnp.dot(left, side(x), preferred_element_type=F32))


def swap(x):
    return pltpu.roll(x, HALF, 1)


def edge_inner(ref):
    a, b = ref[:, :LANES], ref[:, LANES:]
    low = lax.broadcasted_iota(jnp.int32, a.shape, 1) < HALF
    return jnp.where(low, a, b), swap(jnp.where(low, b, a))


def lane_take(src, lane):
    return jnp.take_along_axis(src, lane, axis=1)


def row_take(ref, row, index):
    got = jnp.zeros(index.shape, jnp.int32)
    width = ref.shape[1]
    for first in range(0, width, LANES):
        size = min(LANES, width - first)
        line = ref[row:row + 1, first:first + size]
        if size < LANES:
            line = jnp.concatenate([line, jnp.zeros((1, LANES - size), jnp.int32)], axis=1)
        tile = jnp.broadcast_to(line, index.shape)
        found = lane_take(tile, index & (LANES - 1))
        got = jnp.where((index >> 7) == first // LANES, found, got)
    return got


def octant_dot(left, x, octant):
    parts = [jnp.where(octant == o, x, 0.0) for o in range(left.shape[1] // x.shape[0])]
    return times(left, jnp.concatenate(parts, axis=0))


def slots_of(parent):
    ids = lax.broadcasted_iota(jnp.int32, (LANES, LANES), 0)
    return jnp.where(ids == parent, 1.0, 0.0).astype(BF16)


NT = (((1,), (1,)), ((), ()))


def gather_sum(mapped, slots):
    r = lax.dot_general(stack(mapped), slots, NT, preferred_element_type=F32)
    n = mapped.shape[0]
    return r[:n] + r[n:]


def kernel(
    curves, groups,
    rhs_ref, start_ref, level_ref, nbr_ref, kind_ref, own0_ref, own1_ref, own2_ref, own3_ref,
    cnbr_ref, ckind_ref, clevel_ref, stiff_ref, smooth_ref, coup_ref, restr_ref,
    out_ref,
    cst, gst, rst, rtst, sst, pk, cnb, ckd, clv, cfield, crow,
    edge_out, from_prev, from_next, part, gpart, hpart,
    esend, erecv, gsend, grecv, hsend, hrecv,
):
    me_c, me_g = lax.axis_index("curve"), lax.axis_index("group")
    me = me_c * groups + me_g
    total = curves * groups
    has_prev, has_next = me > 0, me < total - 1
    prev_id = ((me - 1) // groups, lax.rem(me + groups - 1, groups))
    next_id = ((me + 1) // groups, lax.rem(me + 1, groups))
    kinds_n = coup_ref.shape[0]
    vals = rhs_ref.shape[0]
    per_one = HALF
    per_three = own3_ref.shape[1] // curves
    per_four = cnbr_ref.shape[1] // curves
    ctiles = cfield.shape[0]

    @pl.when(jnp.logical_not(has_prev))
    def _():
        from_prev[...] = jnp.zeros_like(from_prev)

    @pl.when(jnp.logical_not(has_next))
    def _():
        from_next[...] = jnp.zeros_like(from_next)

    start_e, start_i = edge_inner(start_ref)
    edge_out[0] = start_e
    barrier = pltpu.get_barrier_semaphore()

    def greet(where):
        pl.semaphore_signal(barrier, inc=1, device_id=where, device_id_type=MESH)

    @pl.when(has_prev)
    def _():
        greet(prev_id)

    @pl.when(has_next)
    def _():
        greet(next_id)

    def over(count, body):
        if count <= 9:
            for off in range(1, count):
                body(off)
        else:
            def step(off, carry):
                body(off)
                return carry
            lax.fori_loop(1, count, step, 0)

    over(groups, lambda off: greet((me_c, lax.rem(me_g + off, groups))))
    over(curves, lambda off: greet((lax.rem(me_c + off, curves), me_g)))
    pl.semaphore_wait(barrier, groups + curves - 2 + has_prev.astype(jnp.int32) + has_next.astype(jnp.int32))

    def to_prev(r):
        return pltpu.make_async_remote_copy(
            src_ref=edge_out.at[r], dst_ref=from_next.at[r], send_sem=esend.at[r, 0],
            recv_sem=erecv.at[r, 0], device_id=prev_id, device_id_type=MESH)

    def to_next(r):
        return pltpu.make_async_remote_copy(
            src_ref=edge_out.at[r], dst_ref=from_prev.at[r], send_sem=esend.at[r, 1],
            recv_sem=erecv.at[r, 1], device_id=next_id, device_id_type=MESH)

    def send_edges(r):
        @pl.when(has_prev)
        def _():
            to_prev(r).start()

        @pl.when(has_next)
        def _():
            to_next(r).start()

    def halo(r):
        @pl.when(has_next)
        def _():
            to_prev(r).wait_recv()

        @pl.when(has_prev)
        def _():
            to_next(r).wait_recv()

        low = lax.broadcasted_iota(jnp.int32, (vals, LANES), 1) < HALF
        return jnp.where(low, from_next[r], from_prev[r])

    send_edges(0)

    for i in range(cst.shape[1] // LANES):
        two = []
        for t in (2 * i, 2 * i + 1):
            two.append(coup_ref[t] if t < kinds_n else stiff_ref[...] if t == kinds_n else jnp.zeros((vals, vals), F32))
        cst[:, i * LANES:(i + 1) * LANES] = stack(jnp.concatenate(two, axis=1))
    for i in range(rst.shape[1] // LANES):
        one, two = restr_ref[2 * i], restr_ref[2 * i + 1]
        cols = slice(i * LANES, (i + 1) * LANES)
        rst[:, cols] = stack(jnp.concatenate([one, two], axis=1))
        rtst[:, cols] = stack(jnp.concatenate([one.T, two.T], axis=1))
    sst[...] = stack(smooth_ref[...])
    pad = gst.shape[0] - (kinds_n + 1) * vals
    if pad:
        gst[(kinds_n + 1) * vals:, :] = jnp.zeros((pad, 2 * LANES), BF16)

    rhs_e, rhs_i = edge_inner(rhs_ref)
    lev_e, lev_i = edge_inner(level_ref)
    scl_e, scl_i = jnp.exp2(lev_e.astype(F32)), jnp.exp2(lev_i.astype(F32))
    gs_e, gs_i = rhs_e * scl_e, rhs_i * scl_i
    nbr_e, nbr_i = edge_inner(nbr_ref)
    kind_e, kind_i = edge_inner(kind_ref)
    lane8 = lax.broadcasted_iota(jnp.int32, (8, LANES), 1)
    at_i = jnp.where(nbr_i != 0, lane8 + HALF + nbr_i, -1000)
    at_e = jnp.where(nbr_e != 0, jnp.where(lane8 < HALF, lane8, lane8 + LANES) + nbr_e, -1000)
    kind_e = jnp.where(nbr_e != 0, kind_e, -1)
    kind_i = jnp.where(nbr_i != 0, kind_i, -1)

    def couple(own, kinds, picks):
        for k in range(kinds.shape[0]):
            pk[k] = picks(k)

        def one(t):
            acc = jnp.where(kinds[0:1] == t, pk[0], 0.0)
            for k in range(1, kinds.shape[0]):
                acc = acc + jnp.where(kinds[k:k + 1] == t, pk[k], 0.0)
            first = t * vals if isinstance(t, int) else pl.multiple_of(t * vals, vals)
            gst[pl.ds(first, vals), :] = side(acc)

        def body(i, carry):
            one(2 * i)
            one(2 * i + 1)
            return carry

        lax.fori_loop(0, kinds_n // 2, body, 0)
        if kinds_n % 2:
            one(kinds_n - 1)
        gst[kinds_n * vals:(kinds_n + 1) * vals, :] = side(own)
        return fold(jnp.dot(cst[...], gst[...], preferred_element_type=F32))

    def wide(row):
        return jnp.broadcast_to(row, (vals, LANES))

    def inner_image(e, i):
        def picks(k):
            at = wide(at_i[k:k + 1])
            lane = at & (LANES - 1)
            is_inner = (at >= HALF) & (at < HALF + LANES)
            return jnp.where(is_inner, lane_take(i, lane ^ HALF), lane_take(e, lane))
        return couple(i, kind_i, picks)

    def edge_image(e, i, h):
        def picks(k):
            at = wide(at_e[k:k + 1])
            lane = at & (LANES - 1)
            is_inner = (at >= HALF) & (at < HALF + LANES)
            is_own = (at >= 0) & (at < 2 * LANES)
            got = jnp.where(is_own, lane_take(e, lane), lane_take(h, lane))
            return jnp.where(is_inner, lane_take(i, lane ^ HALF), got)
        return couple(e, kind_e, picks)

    def smooth(v, gs, image):
        return v + DAMPING * times(sst[...], gs - image)

    e, i = start_e, start_i
    for r in range(2):
        new_i = smooth(i, gs_i, inner_image(e, i))
        new_e = smooth(e, gs_e, edge_image(e, i, halo(r)))
        e, i = new_e, new_i
        edge_out[r + 1] = e
        send_edges(r + 1)
    res_i = rhs_i - inner_image(e, i) / scl_i
    res_e = rhs_e - edge_image(e, i, halo(2)) / scl_e

    lane_at = lane8
    own0_e, own0_i = edge_inner(own0_ref)
    at_one = jnp.where(lane_at < per_one, me_g * per_one + lane_at, 0)
    par1, oct1 = row_take(own1_ref, 0, at_one), row_take(own1_ref, 1, at_one)
    at_two = jnp.where(lane_at < own2_ref.shape[1], lane_at, 0)
    par2, oct2 = row_take(own2_ref, 0, at_two), row_take(own2_ref, 1, at_two)
    at_three = jnp.where(lane_at < per_three, me_c * per_three + lane_at, 0)
    par3, oct3 = row_take(own3_ref, 0, at_three), row_take(own3_ref, 1, at_three)

    one = (gather_sum(octant_dot(rst[...], res_e, own0_e[1:2]), slots_of(own0_e[0:1]))
           + gather_sum(octant_dot(rst[...], res_i, own0_i[1:2]), slots_of(own0_i[0:1])))
    two = gather_sum(octant_dot(rst[...], one, oct1[0:1]), slots_of(par1[0:1]))
    three = gather_sum(octant_dot(rst[...], two, oct2[0:1]), slots_of(par2[0:1]))
    mapped = octant_dot(rst[...], three, oct3[0:1])
    ids = lax.broadcasted_iota(jnp.int32, (8, LANES), 0)
    slots = jnp.where(ids == par3[0:1], 1.0, 0.0).astype(BF16)
    hi, lo = split(mapped)
    zeros = jnp.zeros_like(hi)
    part[...] = (lax.dot_general(slots, jnp.concatenate([hi, zeros], axis=0), NT, preferred_element_type=F32)
                 + lax.dot_general(slots, jnp.concatenate([lo, zeros], axis=0), NT, preferred_element_type=F32))

    def to_group(off):
        return pltpu.make_async_remote_copy(
            src_ref=part, dst_ref=gpart.at[off], send_sem=gsend.at[off], recv_sem=grecv.at[off],
            device_id=(me_c, lax.rem(me_g + off, groups)), device_id_type=MESH)

    def to_curve(off):
        return pltpu.make_async_remote_copy(
            src_ref=hpart.at[me_c], dst_ref=hpart.at[me_c], send_sem=hsend.at[off], recv_sem=hrecv.at[off],
            device_id=(lax.rem(me_c + off, curves), me_g), device_id_type=MESH)

    def from_curve(off):
        who = lax.rem(me_c + curves - off, curves)
        return pltpu.make_async_remote_copy(
            src_ref=hpart.at[who], dst_ref=hpart.at[who], send_sem=hsend.at[off], recv_sem=hrecv.at[off],
            device_id=(lax.rem(me_c + off, curves), me_g), device_id_type=MESH)

    over(groups, lambda off: to_group(off).start())
    over(groups, lambda off: to_group(off).wait_recv())
    mine = part[...]
    for off in range(1, groups):
        mine = mine + gpart[off]
    hpart[me_c] = mine
    over(curves, lambda off: to_curve(off).start())
    cnb[...] = jnp.full_like(cnb, -1)
    ckd[...] = jnp.full_like(ckd, -1)
    clv[...] = jnp.zeros_like(clv)
    crow[...] = jnp.zeros_like(crow)
    width = cnbr_ref.shape[1]
    cnb[:, :width] = cnbr_ref[...]
    ckd[:, :width] = ckind_ref[...]
    clv[:, :width] = jnp.broadcast_to(clevel_ref[...], (8, width))
    over(curves, lambda off: from_curve(off).wait_recv())

    for m in range(curves):
        crow[m * per_four:(m + 1) * per_four, :] = hpart[m, :per_four, :]
    crhs = []
    for n in range(ctiles):
        cols = slice(n * LANES, (n + 1) * LANES)
        block = crow[cols, :].T[:vals]
        crhs.append(block * jnp.exp2(clv[0:1, cols].astype(F32)))
    field = [DAMPING * times(sst[...], g) for g in crhs]
    for sweep in range(COARSE_SWEEPS - 1):
        new = []
        for n in range(ctiles):
            cols = slice(n * LANES, (n + 1) * LANES)
            at_c = cnb[:, cols]
            kind_c = jnp.where(at_c >= 0, ckd[:, cols], -1)

            def picks(k, at_c=at_c):
                at = wide(at_c[k:k + 1])
                lane = at & (LANES - 1)
                got = lane_take(field[0], lane)
                for s in range(1, ctiles):
                    got = jnp.where((at >> 7) == s, lane_take(field[s], lane), got)
                return got

            new.append(smooth(field[n], crhs[n], couple(field[n], kind_c, picks)))
        field = new

    at = wide(jnp.where(lane_at < per_three, me_c * per_four + par3, 0)[0:1])
    back = lane_take(field[0], at & (LANES - 1))
    for s in range(1, ctiles):
        back = jnp.where((at >> 7) == s, lane_take(field[s], at & (LANES - 1)), back)
    back = octant_dot(rtst[...], back, oct3[0:1])
    back = octant_dot(rtst[...], lane_take(back, wide(par2[0:1])), oct2[0:1])
    back = octant_dot(rtst[...], lane_take(back, wide(par1[0:1])), oct1[0:1])
    e = e + octant_dot(rtst[...], lane_take(back, wide(own0_e[0:1])), own0_e[1:2])
    edge_out[3] = e
    send_edges(3)
    i = i + octant_dot(rtst[...], lane_take(back, wide(own0_i[0:1])), own0_i[1:2])

    new_i = smooth(i, gs_i, inner_image(e, i))
    new_e = smooth(e, gs_e, edge_image(e, i, halo(3)))
    low = lax.broadcasted_iota(jnp.int32, (vals, LANES), 1) < HALF
    turned = swap(new_i)
    out_ref[:, :LANES] = jnp.where(low, new_e, turned)
    out_ref[:, LANES:] = jnp.where(low, turned, new_e)

    over(groups, lambda off: to_group(off).wait_send())
    over(curves, lambda off: to_curve(off).wait_send())

    @pl.when(has_prev)
    def _():
        for r in range(4):
            to_prev(r).wait_send()

    @pl.when(has_next)
    def _():
        for r in range(4):
            to_next(r).wait_send()


def solution(mesh):
    curves, groups = mesh.shape["curve"], mesh.shape["group"]

    def shards(*args):
        args = list(args)
        args[2] = args[2].reshape(1, -1)
        args[11] = args[11].reshape(1, -1)
        rhs, coup, restr = args[0], args[14], args[15]
        vals, blocks = rhs.shape
        kinds = coup.shape[0] + 1
        depth = (kinds + kinds % 2) * vals
        cw = -(-args[9].shape[1] // LANES) * LANES
        rdepth = restr.shape[0] * vals
        assert blocks == 2 * LANES and vals == HALF
        vm = pltpu.VMEM
        return pl.pallas_call(
            functools.partial(kernel, curves, groups),
            out_shape=jax.ShapeDtypeStruct(rhs.shape, F32),
            in_specs=[pl.BlockSpec(memory_space=pltpu.VMEM)] * len(args),
            out_specs=pl.BlockSpec(memory_space=pltpu.VMEM),
            scratch_shapes=[
                vm((2 * vals, depth), BF16),
                vm((depth, 2 * LANES), BF16),
                vm((2 * vals, rdepth), BF16),
                vm((2 * vals, rdepth), BF16),
                vm((2 * vals, vals), BF16),
                vm((8, vals, LANES), F32),
                vm((8, cw), jnp.int32),
                vm((8, cw), jnp.int32),
                vm((8, cw), jnp.int32),
                vm((cw // LANES, vals, LANES), F32),
                vm((cw, LANES), F32),
                vm((4, vals, LANES), F32),
                vm((4, vals, LANES), F32),
                vm((4, vals, LANES), F32),
                vm((8, LANES), F32),
                vm((groups, 8, LANES), F32),
                vm((curves, 8, LANES), F32),
                pltpu.SemaphoreType.DMA((4, 2)),
                pltpu.SemaphoreType.DMA((4, 2)),
                pltpu.SemaphoreType.DMA((groups,)),
                pltpu.SemaphoreType.DMA((groups,)),
                pltpu.SemaphoreType.DMA((curves,)),
                pltpu.SemaphoreType.DMA((curves,)),
            ],
            compiler_params=pltpu.CompilerParams(
                collective_id=0, has_side_effects=True, vmem_limit_bytes=32 * 2**20
            ),
        )(*args)

    fine, part, all_ = P(None, ("curve", "group")), P(None, "curve"), P()
    return jax.shard_map(
        shards,
        mesh=mesh,
        in_specs=(fine, fine, P(("curve", "group")), fine, fine, fine, part, part) + (all_,) * 8,
        out_specs=fine,
        check_vma=False,
    )
```

```python
import functools

import jax
import jax.numpy as jnp
from jax import lax
from jax.experimental import pallas as pl
from jax.experimental.pallas import tpu as pltpu
from jax.sharding import PartitionSpec as P

DAMPING = 0.7
COARSE_SWEEPS = 3
LANES = 128
HALF = 64
F32, BF16 = jnp.float32, jnp.bfloat16
MESH = pl.DeviceIdType.MESH


def split(x):
    hi = x.astype(BF16)
    return hi, (x - hi.astype(F32)).astype(BF16)


def stack(x):
    return jnp.concatenate(split(x), axis=0)


def side(x):
    return jnp.concatenate(split(x), axis=1)


def fold(r):
    n = r.shape[0] // 2
    return (r[:n, :LANES] + r[n:, :LANES]) + r[:n, LANES:]


def times(left, x):
    return fold(jnp.dot(left, side(x), preferred_element_type=F32))


def swap(x):
    return pltpu.roll(x, HALF, 1)


def edge_inner(ref):
    a, b = ref[:, :LANES], ref[:, LANES:]
    low = lax.broadcasted_iota(jnp.int32, a.shape, 1) < HALF
    return jnp.where(low, a, b), swap(jnp.where(low, b, a))


def lane_take(src, lane):
    return jnp.take_along_axis(src, lane, axis=1)


def row_take(ref, row, index):
    got = jnp.zeros(index.shape, jnp.int32)
    width = ref.shape[1]
    for first in range(0, width, LANES):
        size = min(LANES, width - first)
        line = ref[row:row + 1, first:first + size]
        if size < LANES:
            line = jnp.concatenate([line, jnp.zeros((1, LANES - size), jnp.int32)], axis=1)
        tile = jnp.broadcast_to(line, index.shape)
        found = lane_take(tile, index & (LANES - 1))
        got = jnp.where((index >> 7) == first // LANES, found, got)
    return got


def octant_dot(left, x, octant):
    n = x.shape[0]
    whole = stack(x)
    code = jnp.broadcast_to(octant.astype(F32), whole.shape).astype(BF16)
    parts = [jnp.where(code == jnp.asarray(o, BF16), whole, jnp.zeros_like(whole)) for o in range(left.shape[1] // n)]
    high = jnp.concatenate([p[:n] for p in parts], axis=0)
    low = jnp.concatenate([p[n:] for p in parts], axis=0)
    return fold(jnp.dot(left, jnp.concatenate([high, low], axis=1), preferred_element_type=F32))


def slots_of(parent):
    ids = lax.broadcasted_iota(jnp.int32, (LANES, LANES), 0)
    return jnp.where(ids == parent, 1.0, 0.0).astype(BF16)


NT = (((1,), (1,)), ((), ()))


def gather_sum(mapped, slots):
    r = lax.dot_general(stack(mapped), slots, NT, preferred_element_type=F32)
    n = mapped.shape[0]
    return r[:n] + r[n:]


def kernel(
    curves, groups, n_in, *refs
):
    held, done = refs[n_in + 1:2 * n_in + 1], refs[2 * n_in + 1]
    loads = [pltpu.make_async_copy(refs[n], held[n], done.at[n]) for n in range(n_in)]
    for n in (1, 0) + tuple(range(2, n_in)):
        loads[n].start()
    cycle(curves, groups, loads, *held, refs[n_in], *refs[2 * n_in + 2:])


def cycle(
    curves, groups, loads,
    rhs_ref, start_ref, level_ref, nbr_ref, kind_ref, own0_ref, own1_ref, own2_ref, own3_ref,
    cnbr_ref, ckind_ref, clevel_ref, stiff_ref, smooth_ref, coup_ref, restr_ref,
    out_ref,
    cst, mst, gst, rst, rtst, sst, cnb, ckd, clv, cfield, crow,
    edge_out, from_prev, from_next, part, gpart, hpart,
    esend, erecv, gsend, grecv, hsend, hrecv,
):
    me_c, me_g = lax.axis_index("curve"), lax.axis_index("group")
    me = me_c * groups + me_g
    total = curves * groups
    has_prev, has_next = me > 0, me < total - 1
    prev_id = ((me - 1) // groups, lax.rem(me + groups - 1, groups))
    next_id = ((me + 1) // groups, lax.rem(me + 1, groups))
    kinds_n = coup_ref.shape[0]
    vals = rhs_ref.shape[0]
    per_one = HALF
    per_three = own3_ref.shape[1] // curves
    per_four = cnbr_ref.shape[1] // curves
    ctiles = cfield.shape[0]

    @pl.when(jnp.logical_not(has_prev))
    def _():
        from_prev[...] = jnp.zeros_like(from_prev)

    @pl.when(jnp.logical_not(has_next))
    def _():
        from_next[...] = jnp.zeros_like(from_next)

    barrier = pltpu.get_barrier_semaphore()

    def greet(where):
        pl.semaphore_signal(barrier, inc=1, device_id=where, device_id_type=MESH)

    @pl.when(has_prev)
    def _():
        greet(prev_id)

    @pl.when(has_next)
    def _():
        greet(next_id)

    def over(count, body):
        if count <= 9:
            for off in range(1, count):
                body(off)
        else:
            def step(off, carry):
                body(off)
                return carry
            lax.fori_loop(1, count, step, 0)

    over(groups, lambda off: greet((me_c, lax.rem(me_g + off, groups))))
    over(curves, lambda off: greet((lax.rem(me_c + off, curves), me_g)))
    loads[1].wait()
    start_e, start_i = edge_inner(start_ref)
    edge_out[0] = start_e
    pl.semaphore_wait(barrier, groups + curves - 2 + has_prev.astype(jnp.int32) + has_next.astype(jnp.int32))

    def to_prev(r):
        return pltpu.make_async_remote_copy(
            src_ref=edge_out.at[r], dst_ref=from_next.at[r], send_sem=esend.at[r, 0],
            recv_sem=erecv.at[r, 0], device_id=prev_id, device_id_type=MESH)

    def to_next(r):
        return pltpu.make_async_remote_copy(
            src_ref=edge_out.at[r], dst_ref=from_prev.at[r], send_sem=esend.at[r, 1],
            recv_sem=erecv.at[r, 1], device_id=next_id, device_id_type=MESH)

    def send_edges(r):
        @pl.when(has_prev)
        def _():
            to_prev(r).start()

        @pl.when(has_next)
        def _():
            to_next(r).start()

    def halo(r):
        @pl.when(has_next)
        def _():
            to_prev(r).wait_recv()

        @pl.when(has_prev)
        def _():
            to_next(r).wait_recv()

        low = lax.broadcasted_iota(jnp.int32, (vals, LANES), 1) < HALF
        return jnp.where(low, from_next[r], from_prev[r])

    send_edges(0)
    for n, load in enumerate(loads):
        if n != 1:
            load.wait()

    sst[...] = stack(DAMPING * smooth_ref[...])
    for i in range(cst.shape[1] // LANES):
        two = []
        for t in (2 * i, 2 * i + 1):
            two.append(coup_ref[t] if t < kinds_n else stiff_ref[...] if t == kinds_n else jnp.zeros((vals, vals), F32))
        both = jnp.concatenate(two, axis=1)
        cst[:, i * LANES:(i + 1) * LANES] = stack(both)
        mst[:, i * LANES:(i + 1) * LANES] = stack(times(sst[...], both))
    for i in range(rst.shape[1] // LANES):
        one, two = restr_ref[2 * i], restr_ref[2 * i + 1]
        cols = slice(i * LANES, (i + 1) * LANES)
        rst[:, cols] = stack(jnp.concatenate([one, two], axis=1))
        rtst[:, cols] = stack(jnp.concatenate([one.T, two.T], axis=1))
    pad = gst.shape[0] - (kinds_n + 1) * vals
    if pad:
        gst[(kinds_n + 1) * vals:, :] = jnp.zeros((pad, 2 * LANES), BF16)

    rhs_e, rhs_i = edge_inner(rhs_ref)
    lev_e, lev_i = edge_inner(level_ref)
    scl_e, scl_i = jnp.exp2(lev_e.astype(F32)), jnp.exp2(lev_i.astype(F32))
    gs_e, gs_i = rhs_e * scl_e, rhs_i * scl_i
    nbr_e, nbr_i = edge_inner(nbr_ref)
    kind_e, kind_i = edge_inner(kind_ref)
    lane8 = lax.broadcasted_iota(jnp.int32, (8, LANES), 1)
    at_i = jnp.where(nbr_i != 0, lane8 + HALF + nbr_i, -1000)
    at_e = jnp.where(nbr_e != 0, jnp.where(lane8 < HALF, lane8, lane8 + LANES) + nbr_e, -1000)
    kind_e = jnp.where(nbr_e != 0, kind_e, -1)
    kind_i = jnp.where(nbr_i != 0, kind_i, -1)

    def couple(left, own, kinds, picks):
        slots_n = kinds.shape[0]
        picked = [picks(k) for k in range(slots_n)]
        codes, parts = [], []
        for k in range(slots_n):
            whole = picked[k]
            for other in range(k):
                same = kinds[other:other + 1] == kinds[k:k + 1]
                whole = whole + jnp.where(same, picked[other], 0.0)
            parts.append(stack(whole))
            codes.append(jnp.broadcast_to(kinds[k:k + 1].astype(F32), (2 * vals, LANES)).astype(BF16))
        for t in range(kinds_n):
            acc = jnp.zeros_like(parts[0])
            for k in range(slots_n):
                acc = jnp.where(codes[k] == jnp.asarray(t, BF16), parts[k], acc)
            gst[t * vals:(t + 1) * vals, :LANES] = acc[:vals]
            gst[t * vals:(t + 1) * vals, LANES:] = acc[vals:]
        gst[kinds_n * vals:(kinds_n + 1) * vals, :] = side(own)
        return fold(jnp.dot(left[...], gst[...], preferred_element_type=F32))

    def wide(row):
        return jnp.broadcast_to(row, (vals, LANES))

    def inner_image(left, e, i):
        def picks(k):
            at = wide(at_i[k:k + 1])
            lane = at & (LANES - 1)
            is_inner = (at >= HALF) & (at < HALF + LANES)
            return jnp.where(is_inner, lane_take(i, lane ^ HALF), lane_take(e, lane))
        return couple(left, i, kind_i, picks)

    def edge_image(left, e, i, h):
        def picks(k):
            at = wide(at_e[k:k + 1])
            lane = at & (LANES - 1)
            is_inner = (at >= HALF) & (at < HALF + LANES)
            is_own = (at >= 0) & (at < 2 * LANES)
            got = jnp.where(is_own, lane_take(e, lane), lane_take(h, lane))
            return jnp.where(is_inner, lane_take(i, lane ^ HALF), got)
        return couple(left, e, kind_e, picks)

    def smooth(v, moved, image):
        return v + (moved - image)

    gs_e, gs_i = times(sst[...], gs_e), times(sst[...], gs_i)

    e, i = start_e, start_i
    for r in range(2):
        new_i = smooth(i, gs_i, inner_image(mst, e, i))
        new_e = smooth(e, gs_e, edge_image(mst, e, i, halo(r)))
        e, i = new_e, new_i
        edge_out[r + 1] = e
        send_edges(r + 1)
    res_i = rhs_i - inner_image(cst, e, i) / scl_i
    res_e = rhs_e - edge_image(cst, e, i, halo(2)) / scl_e

    lane_at = lane8
    own0_e, own0_i = edge_inner(own0_ref)
    at_one = jnp.where(lane_at < per_one, me_g * per_one + lane_at, 0)
    par1, oct1 = row_take(own1_ref, 0, at_one), row_take(own1_ref, 1, at_one)
    at_two = jnp.where(lane_at < own2_ref.shape[1], lane_at, 0)
    par2, oct2 = row_take(own2_ref, 0, at_two), row_take(own2_ref, 1, at_two)
    at_three = jnp.where(lane_at < per_three, me_c * per_three + lane_at, 0)
    par3, oct3 = row_take(own3_ref, 0, at_three), row_take(own3_ref, 1, at_three)

    one = (gather_sum(octant_dot(rst[...], res_e, own0_e[1:2]), slots_of(own0_e[0:1]))
           + gather_sum(octant_dot(rst[...], res_i, own0_i[1:2]), slots_of(own0_i[0:1])))
    two = gather_sum(octant_dot(rst[...], one, oct1[0:1]), slots_of(par1[0:1]))
    three = gather_sum(octant_dot(rst[...], two, oct2[0:1]), slots_of(par2[0:1]))
    mapped = octant_dot(rst[...], three, oct3[0:1])
    ids = lax.broadcasted_iota(jnp.int32, (8, LANES), 0)
    slots = jnp.where(ids == par3[0:1], 1.0, 0.0).astype(BF16)
    hi, lo = split(mapped)
    zeros = jnp.zeros_like(hi)
    part[...] = (lax.dot_general(slots, jnp.concatenate([hi, zeros], axis=0), NT, preferred_element_type=F32)
                 + lax.dot_general(slots, jnp.concatenate([lo, zeros], axis=0), NT, preferred_element_type=F32))

    def to_group(off):
        return pltpu.make_async_remote_copy(
            src_ref=part, dst_ref=gpart.at[off], send_sem=gsend.at[off], recv_sem=grecv.at[off],
            device_id=(me_c, lax.rem(me_g + off, groups)), device_id_type=MESH)

    def to_curve(off):
        return pltpu.make_async_remote_copy(
            src_ref=hpart.at[me_c], dst_ref=hpart.at[me_c], send_sem=hsend.at[off], recv_sem=hrecv.at[off],
            device_id=(lax.rem(me_c + off, curves), me_g), device_id_type=MESH)

    def from_curve(off):
        who = lax.rem(me_c + curves - off, curves)
        return pltpu.make_async_remote_copy(
            src_ref=hpart.at[who], dst_ref=hpart.at[who], send_sem=hsend.at[off], recv_sem=hrecv.at[off],
            device_id=(lax.rem(me_c + off, curves), me_g), device_id_type=MESH)

    over(groups, lambda off: to_group(off).start())
    over(groups, lambda off: to_group(off).wait_recv())
    mine = part[...]
    for off in range(1, groups):
        mine = mine + gpart[off]
    hpart[me_c] = mine
    over(curves, lambda off: to_curve(off).start())
    cnb[...] = jnp.full_like(cnb, -1)
    ckd[...] = jnp.full_like(ckd, -1)
    clv[...] = jnp.zeros_like(clv)
    crow[...] = jnp.zeros_like(crow)
    width = cnbr_ref.shape[1]
    cnb[:, :width] = cnbr_ref[...]
    ckd[:, :width] = ckind_ref[...]
    clv[:, :width] = jnp.broadcast_to(clevel_ref[...], (8, width))
    over(curves, lambda off: from_curve(off).wait_recv())

    for m in range(curves):
        crow[m * per_four:(m + 1) * per_four, :] = hpart[m, :per_four, :]
    crhs = []
    for n in range(ctiles):
        cols = slice(n * LANES, (n + 1) * LANES)
        block = crow[cols, :].T[:vals]
        crhs.append(times(sst[...], block * jnp.exp2(clv[0:1, cols].astype(F32))))
    field = crhs
    for sweep in range(COARSE_SWEEPS - 1):
        new = []
        for n in range(ctiles):
            cols = slice(n * LANES, (n + 1) * LANES)
            at_c = cnb[:, cols]
            kind_c = jnp.where(at_c >= 0, ckd[:, cols], -1)

            def picks(k, at_c=at_c):
                at = wide(at_c[k:k + 1])
                lane = at & (LANES - 1)
                got = lane_take(field[0], lane)
                for s in range(1, ctiles):
                    got = jnp.where((at >> 7) == s, lane_take(field[s], lane), got)
                return got

            new.append(smooth(field[n], crhs[n], couple(mst, field[n], kind_c, picks)))
        field = new

    at = wide(jnp.where(lane_at < per_three, me_c * per_four + par3, 0)[0:1])
    back = lane_take(field[0], at & (LANES - 1))
    for s in range(1, ctiles):
        back = jnp.where((at >> 7) == s, lane_take(field[s], at & (LANES - 1)), back)
    back = octant_dot(rtst[...], back, oct3[0:1])
    back = octant_dot(rtst[...], lane_take(back, wide(par2[0:1])), oct2[0:1])
    back = octant_dot(rtst[...], lane_take(back, wide(par1[0:1])), oct1[0:1])
    e = e + octant_dot(rtst[...], lane_take(back, wide(own0_e[0:1])), own0_e[1:2])
    edge_out[3] = e
    send_edges(3)
    i = i + octant_dot(rtst[...], lane_take(back, wide(own0_i[0:1])), own0_i[1:2])

    new_i = smooth(i, gs_i, inner_image(mst, e, i))
    new_e = smooth(e, gs_e, edge_image(mst, e, i, halo(3)))
    low = lax.broadcasted_iota(jnp.int32, (vals, LANES), 1) < HALF
    turned = swap(new_i)
    out_ref[:, :LANES] = jnp.where(low, new_e, turned)
    out_ref[:, LANES:] = jnp.where(low, turned, new_e)

    over(groups, lambda off: to_group(off).wait_send())
    over(curves, lambda off: to_curve(off).wait_send())

    @pl.when(has_prev)
    def _():
        for r in range(4):
            to_prev(r).wait_send()

    @pl.when(has_next)
    def _():
        for r in range(4):
            to_next(r).wait_send()


def solution(mesh):
    curves, groups = mesh.shape["curve"], mesh.shape["group"]

    def shards(*args):
        args = list(args)
        args[2] = args[2].reshape(1, -1)
        args[11] = args[11].reshape(1, -1)
        rhs, coup, restr = args[0], args[14], args[15]
        vals, blocks = rhs.shape
        kinds = coup.shape[0] + 1
        depth = (kinds + kinds % 2) * vals
        cw = -(-args[9].shape[1] // LANES) * LANES
        rdepth = restr.shape[0] * vals
        assert blocks == 2 * LANES and vals == HALF
        vm = pltpu.VMEM
        return pl.pallas_call(
            functools.partial(kernel, curves, groups, len(args)),
            out_shape=jax.ShapeDtypeStruct(rhs.shape, F32),
            in_specs=[pl.BlockSpec(memory_space=pltpu.HBM)] * len(args),
            out_specs=pl.BlockSpec(memory_space=pltpu.VMEM),
            scratch_shapes=[vm(a.shape, a.dtype) for a in args] + [
                pltpu.SemaphoreType.DMA((len(args),)),
                vm((2 * vals, depth), BF16),
                vm((2 * vals, depth), BF16),
                vm((depth, 2 * LANES), BF16),
                vm((2 * vals, rdepth), BF16),
                vm((2 * vals, rdepth), BF16),
                vm((2 * vals, vals), BF16),
                vm((8, cw), jnp.int32),
                vm((8, cw), jnp.int32),
                vm((8, cw), jnp.int32),
                vm((cw // LANES, vals, LANES), F32),
                vm((cw, LANES), F32),
                vm((4, vals, LANES), F32),
                vm((4, vals, LANES), F32),
                vm((4, vals, LANES), F32),
                vm((8, LANES), F32),
                vm((groups, 8, LANES), F32),
                vm((curves, 8, LANES), F32),
                pltpu.SemaphoreType.DMA((4, 2)),
                pltpu.SemaphoreType.DMA((4, 2)),
                pltpu.SemaphoreType.DMA((groups,)),
                pltpu.SemaphoreType.DMA((groups,)),
                pltpu.SemaphoreType.DMA((curves,)),
                pltpu.SemaphoreType.DMA((curves,)),
            ],
            compiler_params=pltpu.CompilerParams(
                collective_id=0, has_side_effects=True, vmem_limit_bytes=60 * 2**20
            ),
        )(*args)

    fine, part, all_ = P(None, ("curve", "group")), P(None, "curve"), P()
    return jax.shard_map(
        shards,
        mesh=mesh,
        in_specs=(fine, fine, P(("curve", "group")), fine, fine, fine, part, part) + (all_,) * 8,
        out_specs=fine,
        check_vma=False,
    )
```

```python
import functools

import jax
import jax.numpy as jnp
from jax import lax
from jax.experimental import pallas as pl
from jax.experimental.pallas import tpu as pltpu
from jax.sharding import PartitionSpec as P

DAMPING = 0.7
COARSE_SWEEPS = 3
LANES = 128
HALF = 64
F32, BF16 = jnp.float32, jnp.bfloat16
MESH = pl.DeviceIdType.MESH


def split(x):
    hi = x.astype(BF16)
    return hi, (x - hi.astype(F32)).astype(BF16)


def stack(x):
    return jnp.concatenate(split(x), axis=0)


def side(x):
    return jnp.concatenate(split(x), axis=1)


def fold(r):
    n = r.shape[0] // 2
    return (r[:n, :LANES] + r[n:, :LANES]) + r[:n, LANES:]


def times(left, x):
    return fold(jnp.dot(left, side(x), preferred_element_type=F32))


def swap(x):
    return pltpu.roll(x, HALF, 1)


def edge_inner(ref):
    a, b = ref[:, :LANES], ref[:, LANES:]
    low = lax.broadcasted_iota(jnp.int32, a.shape, 1) < HALF
    return jnp.where(low, a, b), swap(jnp.where(low, b, a))


def lane_take(src, lane):
    return jnp.take_along_axis(src, lane, axis=1)


def row_take(ref, row, index):
    got = jnp.zeros(index.shape, jnp.int32)
    width = ref.shape[1]
    for first in range(0, width, LANES):
        size = min(LANES, width - first)
        line = ref[row:row + 1, first:first + size]
        if size < LANES:
            line = jnp.concatenate([line, jnp.zeros((1, LANES - size), jnp.int32)], axis=1)
        tile = jnp.broadcast_to(line, index.shape)
        found = lane_take(tile, index & (LANES - 1))
        got = jnp.where((index >> 7) == first // LANES, found, got)
    return got


def octant_dot(left, x, octant):
    n = x.shape[0]
    whole = stack(x)
    code = jnp.broadcast_to(octant.astype(F32), whole.shape).astype(BF16)
    parts = [jnp.where(code == jnp.asarray(o, BF16), whole, jnp.zeros_like(whole)) for o in range(left.shape[1] // n)]
    high = jnp.concatenate([p[:n] for p in parts], axis=0)
    low = jnp.concatenate([p[n:] for p in parts], axis=0)
    return fold(jnp.dot(left, jnp.concatenate([high, low], axis=1), preferred_element_type=F32))


def slots_of(parent):
    ids = lax.broadcasted_iota(jnp.int32, (LANES, LANES), 0)
    return jnp.where(ids == parent, 1.0, 0.0).astype(BF16)


NT = (((1,), (1,)), ((), ()))


def gather_sum(mapped, slots):
    r = lax.dot_general(stack(mapped), slots, NT, preferred_element_type=F32)
    n = mapped.shape[0]
    return r[:n] + r[n:]


def kernel(
    curves, groups, n_in, *refs
):
    held, done = refs[n_in + 2:2 * n_in + 2], refs[2 * n_in + 2]
    loads = [pltpu.make_async_copy(refs[n], held[n], done.at[n]) for n in range(n_in)]
    for n in (1, 0) + tuple(range(2, n_in)):
        loads[n].start()
    cycle(curves, groups, loads, *held, *refs[n_in:n_in + 2], *refs[2 * n_in + 3:])


def cycle(
    curves, groups, loads,
    rhs_ref, start_ref, level_ref, nbr_ref, kind_ref, own0_ref, own1_ref, own2_ref, own3_ref,
    cnbr_ref, ckind_ref, clevel_ref, stiff_ref, smooth_ref, coup_ref, restr_ref,
    base_ref, step_ref,
    mats, gst, rst, rtst, sst, cnb, ckd, clv, cfield, crhs, crow, cur, res, fix,
    edge_out, from_prev, from_next, part, gpart, hpart,
    esend, erecv, gsend, grecv, hsend, hrecv,
):
    me_c, me_g = lax.axis_index("curve"), lax.axis_index("group")
    me = me_c * groups + me_g
    total = curves * groups
    has_prev, has_next = me > 0, me < total - 1
    prev_id = ((me - 1) // groups, lax.rem(me + groups - 1, groups))
    next_id = ((me + 1) // groups, lax.rem(me + 1, groups))
    kinds_n = coup_ref.shape[0]
    vals = rhs_ref.shape[0]
    per_one = HALF
    per_three = own3_ref.shape[1] // curves
    per_four = cnbr_ref.shape[1] // curves
    ctiles = cfield.shape[1]

    @pl.when(jnp.logical_not(has_prev))
    def _():
        from_prev[...] = jnp.zeros_like(from_prev)

    @pl.when(jnp.logical_not(has_next))
    def _():
        from_next[...] = jnp.zeros_like(from_next)

    barrier = pltpu.get_barrier_semaphore()

    def greet(where):
        pl.semaphore_signal(barrier, inc=1, device_id=where, device_id_type=MESH)

    @pl.when(has_prev)
    def _():
        greet(prev_id)

    @pl.when(has_next)
    def _():
        greet(next_id)

    def over(count, body):
        if count <= 9:
            for off in range(1, count):
                body(off)
        else:
            def step(off, carry):
                body(off)
                return carry
            lax.fori_loop(1, count, step, 0)

    over(groups, lambda off: greet((me_c, lax.rem(me_g + off, groups))))
    over(curves, lambda off: greet((lax.rem(me_c + off, curves), me_g)))
    loads[1].wait()
    start_e, start_i = edge_inner(start_ref)
    edge_out[0] = start_e
    pl.semaphore_wait(barrier, groups + curves - 2 + has_prev.astype(jnp.int32) + has_next.astype(jnp.int32))

    def to_prev(r):
        return pltpu.make_async_remote_copy(
            src_ref=edge_out.at[r], dst_ref=from_next.at[r], send_sem=esend.at[r, 0],
            recv_sem=erecv.at[r, 0], device_id=prev_id, device_id_type=MESH)

    def to_next(r):
        return pltpu.make_async_remote_copy(
            src_ref=edge_out.at[r], dst_ref=from_prev.at[r], send_sem=esend.at[r, 1],
            recv_sem=erecv.at[r, 1], device_id=next_id, device_id_type=MESH)

    def send_edges(r):
        @pl.when(has_prev)
        def _():
            to_prev(r).start()

        @pl.when(has_next)
        def _():
            to_next(r).start()

    def halo(r):
        @pl.when(has_next)
        def _():
            to_prev(r).wait_recv()

        @pl.when(has_prev)
        def _():
            to_next(r).wait_recv()

        low = lax.broadcasted_iota(jnp.int32, (vals, LANES), 1) < HALF
        return jnp.where(low, from_next[r], from_prev[r])

    send_edges(0)
    for n, load in enumerate(loads):
        if n != 1:
            load.wait()

    sst[...] = stack(DAMPING * smooth_ref[...])
    for i in range(mats.shape[2] // LANES):
        two = []
        for t in (2 * i, 2 * i + 1):
            two.append(coup_ref[t] if t < kinds_n else stiff_ref[...] if t == kinds_n else jnp.zeros((vals, vals), F32))
        both = jnp.concatenate(two, axis=1)
        mats[1, :, i * LANES:(i + 1) * LANES] = stack(both)
        mats[0, :, i * LANES:(i + 1) * LANES] = stack(times(sst[...], both))
    for i in range(rst.shape[1] // LANES):
        one, two = restr_ref[2 * i], restr_ref[2 * i + 1]
        cols = slice(i * LANES, (i + 1) * LANES)
        rst[:, cols] = stack(jnp.concatenate([one, two], axis=1))
        rtst[:, cols] = stack(jnp.concatenate([one.T, two.T], axis=1))
    pad = gst.shape[0] - (kinds_n + 1) * vals
    if pad:
        gst[(kinds_n + 1) * vals:, :] = jnp.zeros((pad, 2 * LANES), BF16)

    rhs_e, rhs_i = edge_inner(rhs_ref)
    lev_e, lev_i = edge_inner(level_ref)
    scl_e, scl_i = jnp.exp2(lev_e.astype(F32)), jnp.exp2(lev_i.astype(F32))
    gs_e, gs_i = rhs_e * scl_e, rhs_i * scl_i
    nbr_e, nbr_i = edge_inner(nbr_ref)
    kind_e, kind_i = edge_inner(kind_ref)
    lane8 = lax.broadcasted_iota(jnp.int32, (8, LANES), 1)
    at_i = jnp.where(nbr_i != 0, lane8 + HALF + nbr_i, -1000)
    at_e = jnp.where(nbr_e != 0, jnp.where(lane8 < HALF, lane8, lane8 + LANES) + nbr_e, -1000)
    kind_e = jnp.where(nbr_e != 0, kind_e, -1)
    kind_i = jnp.where(nbr_i != 0, kind_i, -1)

    def couple(left, own, kinds, picks):
        slots_n = kinds.shape[0]
        picked = [picks(k) for k in range(slots_n)]
        codes, parts = [], []
        for k in range(slots_n):
            whole = picked[k]
            for other in range(k):
                same = kinds[other:other + 1] == kinds[k:k + 1]
                whole = whole + jnp.where(same, picked[other], 0.0)
            parts.append(stack(whole))
            codes.append(jnp.broadcast_to(kinds[k:k + 1].astype(F32), (2 * vals, LANES)).astype(BF16))
        for t in range(kinds_n):
            acc = jnp.zeros_like(parts[0])
            for k in range(slots_n):
                acc = jnp.where(codes[k] == jnp.asarray(t, BF16), parts[k], acc)
            gst[t * vals:(t + 1) * vals, :LANES] = acc[:vals]
            gst[t * vals:(t + 1) * vals, LANES:] = acc[vals:]
        gst[kinds_n * vals:(kinds_n + 1) * vals, :] = side(own)
        return fold(jnp.dot(left[...], gst[...], preferred_element_type=F32))

    def wide(row):
        return jnp.broadcast_to(row, (vals, LANES))

    def inner_image(left, e, i):
        def picks(k):
            at = wide(at_i[k:k + 1])
            lane = at & (LANES - 1)
            is_inner = (at >= HALF) & (at < HALF + LANES)
            return jnp.where(is_inner, lane_take(i, lane ^ HALF), lane_take(e, lane))
        return couple(left, i, kind_i, picks)

    def edge_image(left, e, i, h):
        def picks(k):
            at = wide(at_e[k:k + 1])
            lane = at & (LANES - 1)
            is_inner = (at >= HALF) & (at < HALF + LANES)
            is_own = (at >= 0) & (at < 2 * LANES)
            got = jnp.where(is_own, lane_take(e, lane), lane_take(h, lane))
            return jnp.where(is_inner, lane_take(i, lane ^ HALF), got)
        return couple(left, e, kind_e, picks)

    fix[0, 0], fix[0, 1] = times(sst[...], gs_e), times(sst[...], gs_i)
    fix[1, 0], fix[1, 1] = rhs_e, rhs_i
    fix[2, 0] = jnp.broadcast_to(1.0 / scl_e, (vals, LANES))
    fix[2, 1] = jnp.broadcast_to(1.0 / scl_i, (vals, LANES))
    cur[0], cur[1] = start_e, start_i

    lane_at = lane8
    own0_e, own0_i = edge_inner(own0_ref)
    at_one = jnp.where(lane_at < per_one, me_g * per_one + lane_at, 0)
    par1, oct1 = row_take(own1_ref, 0, at_one), row_take(own1_ref, 1, at_one)
    at_two = jnp.where(lane_at < own2_ref.shape[1], lane_at, 0)
    par2, oct2 = row_take(own2_ref, 0, at_two), row_take(own2_ref, 1, at_two)
    at_three = jnp.where(lane_at < per_three, me_c * per_three + lane_at, 0)
    par3, oct3 = row_take(own3_ref, 0, at_three), row_take(own3_ref, 1, at_three)

    width = cnbr_ref.shape[1]
    cnb[...] = jnp.full_like(cnb, -1)
    ckd[...] = jnp.full_like(ckd, -1)
    clv[...] = jnp.zeros_like(clv)
    crow[...] = jnp.zeros_like(crow)
    for n in range(ctiles):
        size = min(LANES, width - n * LANES)
        cols = slice(n * LANES, n * LANES + size)
        cnb[n, :, :size] = cnbr_ref[:, cols]
        ckd[n, :, :size] = ckind_ref[:, cols]
        clv[n, :, :size] = jnp.broadcast_to(clevel_ref[:, cols], (8, size))

    def to_group(off):
        return pltpu.make_async_remote_copy(
            src_ref=part, dst_ref=gpart.at[off], send_sem=gsend.at[off], recv_sem=grecv.at[off],
            device_id=(me_c, lax.rem(me_g + off, groups)), device_id_type=MESH)

    def to_curve(off):
        return pltpu.make_async_remote_copy(
            src_ref=hpart.at[me_c], dst_ref=hpart.at[me_c], send_sem=hsend.at[off], recv_sem=hrecv.at[off],
            device_id=(lax.rem(me_c + off, curves), me_g), device_id_type=MESH)

    def from_curve(off):
        who = lax.rem(me_c + curves - off, curves)
        return pltpu.make_async_remote_copy(
            src_ref=hpart.at[who], dst_ref=hpart.at[who], send_sem=hsend.at[off], recv_sem=hrecv.at[off],
            device_id=(lax.rem(me_c + off, curves), me_g), device_id_type=MESH)

    def middle():
        one = (gather_sum(octant_dot(rst[...], res[0], own0_e[1:2]), slots_of(own0_e[0:1]))
               + gather_sum(octant_dot(rst[...], res[1], own0_i[1:2]), slots_of(own0_i[0:1])))
        two = gather_sum(octant_dot(rst[...], one, oct1[0:1]), slots_of(par1[0:1]))
        three = gather_sum(octant_dot(rst[...], two, oct2[0:1]), slots_of(par2[0:1]))
        mapped = octant_dot(rst[...], three, oct3[0:1])
        ids = lax.broadcasted_iota(jnp.int32, (8, LANES), 0)
        slots = jnp.where(ids == par3[0:1], 1.0, 0.0).astype(BF16)
        hi, lo = split(mapped)
        zeros = jnp.zeros_like(hi)
        part[...] = (lax.dot_general(slots, jnp.concatenate([hi, zeros], axis=0), NT, preferred_element_type=F32)
                     + lax.dot_general(slots, jnp.concatenate([lo, zeros], axis=0), NT, preferred_element_type=F32))

        over(groups, lambda off: to_group(off).start())
        over(groups, lambda off: to_group(off).wait_recv())
        mine = part[...]
        for off in range(1, groups):
            mine = mine + gpart[off]
        hpart[me_c] = mine
        over(curves, lambda off: to_curve(off).start())
        over(curves, lambda off: from_curve(off).wait_recv())

        for m in range(curves):
            crow[m * per_four:(m + 1) * per_four, :] = hpart[m, :per_four, :]
        for n in range(ctiles):
            block = crow[n * LANES:(n + 1) * LANES, :].T[:vals]
            crhs[n] = times(sst[...], block * jnp.exp2(clv[n, 0:1].astype(F32)))
            cfield[0, n] = crhs[n]

        def coarse_step(s, carry):
            sweep, n = s // ctiles, lax.rem(s, ctiles)
            old = lax.rem(sweep, 2)
            at_c = cnb[n]
            kind_c = jnp.where(at_c >= 0, ckd[n], -1)
            field = [cfield[old, m] for m in range(ctiles)]
            own = cfield[old, n]

            def picks(k):
                at = wide(at_c[k:k + 1])
                lane = at & (LANES - 1)
                got = lane_take(field[0], lane)
                for m in range(1, ctiles):
                    got = jnp.where((at >> 7) == m, lane_take(field[m], lane), got)
                return got

            cfield[1 - old, n] = own + (crhs[n] - couple(mats.at[0], own, kind_c, picks))
            return carry

        lax.fori_loop(0, (COARSE_SWEEPS - 1) * ctiles, coarse_step, 0)
        field = [cfield[(COARSE_SWEEPS - 1) % 2, m] for m in range(ctiles)]

        at = wide(jnp.where(lane_at < per_three, me_c * per_four + par3, 0)[0:1])
        back = lane_take(field[0], at & (LANES - 1))
        for s in range(1, ctiles):
            back = jnp.where((at >> 7) == s, lane_take(field[s], at & (LANES - 1)), back)
        back = octant_dot(rtst[...], back, oct3[0:1])
        back = octant_dot(rtst[...], lane_take(back, wide(par2[0:1])), oct2[0:1])
        back = octant_dot(rtst[...], lane_take(back, wide(par1[0:1])), oct1[0:1])
        e = cur[0] + octant_dot(rtst[...], lane_take(back, wide(own0_e[0:1])), own0_e[1:2])
        edge_out[3] = e
        cur[0] = e
        send_edges(3)
        cur[1] = cur[1] + octant_dot(rtst[...], lane_take(back, wide(own0_i[0:1])), own0_i[1:2])

    def sweep(r, carry):
        @pl.when(r == 3)
        def _():
            middle()

        left = mats.at[(r == 2).astype(jnp.int32)]
        inner = inner_image(left, cur[0], cur[1])
        edge = edge_image(left, cur[0], cur[1], halo(r))

        @pl.when(r == 2)
        def _():
            res[0] = fix[1, 0] - edge * fix[2, 0]
            res[1] = fix[1, 1] - inner * fix[2, 1]

        @pl.when(r < 2)
        def _():
            new = cur[0] + (fix[0, 0] - edge)
            cur[0] = new
            cur[1] = cur[1] + (fix[0, 1] - inner)
            edge_out[r + 1] = new
            send_edges(r + 1)

        @pl.when(r == 3)
        def _():
            low = lax.broadcasted_iota(jnp.int32, (vals, LANES), 1) < HALF
            for ref, e, i in ((base_ref, cur[0], cur[1]), (step_ref, fix[0, 0] - edge, fix[0, 1] - inner)):
                turned = swap(i)
                ref[:, :LANES] = jnp.where(low, e, turned)
                ref[:, LANES:] = jnp.where(low, turned, e)

        return carry

    lax.fori_loop(0, 4, sweep, 0)

    over(groups, lambda off: to_group(off).wait_send())
    over(curves, lambda off: to_curve(off).wait_send())

    @pl.when(has_prev)
    def _():
        for r in range(4):
            to_prev(r).wait_send()

    @pl.when(has_next)
    def _():
        for r in range(4):
            to_next(r).wait_send()


def solution(mesh):
    curves, groups = mesh.shape["curve"], mesh.shape["group"]

    def shards(*args):
        args = list(args)
        args[2] = args[2].reshape(1, -1)
        args[11] = args[11].reshape(1, -1)
        rhs, coup, restr = args[0], args[14], args[15]
        vals, blocks = rhs.shape
        kinds = coup.shape[0] + 1
        depth = (kinds + kinds % 2) * vals
        cw = -(-args[9].shape[1] // LANES) * LANES
        rdepth = restr.shape[0] * vals
        assert blocks == 2 * LANES and vals == HALF
        vm = pltpu.VMEM
        base, step = pl.pallas_call(
            functools.partial(kernel, curves, groups, len(args)),
            out_shape=[jax.ShapeDtypeStruct(rhs.shape, F32)] * 2,
            in_specs=[pl.BlockSpec(memory_space=pltpu.HBM)] * len(args),
            out_specs=[pl.BlockSpec(memory_space=pltpu.VMEM)] * 2,
            scratch_shapes=[vm(a.shape, a.dtype) for a in args] + [
                pltpu.SemaphoreType.DMA((len(args),)),
                vm((2, 2 * vals, depth), BF16),
                vm((depth, 2 * LANES), BF16),
                vm((2 * vals, rdepth), BF16),
                vm((2 * vals, rdepth), BF16),
                vm((2 * vals, vals), BF16),
                vm((cw // LANES, 8, LANES), jnp.int32),
                vm((cw // LANES, 8, LANES), jnp.int32),
                vm((cw // LANES, 8, LANES), jnp.int32),
                vm((2, cw // LANES, vals, LANES), F32),
                vm((cw // LANES, vals, LANES), F32),
                vm((cw, LANES), F32),
                vm((2, vals, LANES), F32),
                vm((2, vals, LANES), F32),
                vm((3, 2, vals, LANES), F32),
                vm((4, vals, LANES), F32),
                vm((4, vals, LANES), F32),
                vm((4, vals, LANES), F32),
                vm((8, LANES), F32),
                vm((groups, 8, LANES), F32),
                vm((curves, 8, LANES), F32),
                pltpu.SemaphoreType.DMA((4, 2)),
                pltpu.SemaphoreType.DMA((4, 2)),
                pltpu.SemaphoreType.DMA((groups,)),
                pltpu.SemaphoreType.DMA((groups,)),
                pltpu.SemaphoreType.DMA((curves,)),
                pltpu.SemaphoreType.DMA((curves,)),
            ],
            compiler_params=pltpu.CompilerParams(
                collective_id=0, has_side_effects=True, vmem_limit_bytes=60 * 2**20
            ),
        )(*args)
        return base + step

    fine, part, all_ = P(None, ("curve", "group")), P(None, "curve"), P()
    return jax.shard_map(
        shards,
        mesh=mesh,
        in_specs=(fine, fine, P(("curve", "group")), fine, fine, fine, part, part) + (all_,) * 8,
        out_specs=fine,
        check_vma=False,
    )
```

```python
import functools

import jax
import jax.numpy as jnp
from jax import lax
from jax.experimental import pallas as pl
from jax.experimental.pallas import tpu as pltpu
from jax.sharding import PartitionSpec as P

DAMPING = 0.7
COARSE_SWEEPS = 3
LANES = 128
HALF = 64
F32, BF16 = jnp.float32, jnp.bfloat16
MESH = pl.DeviceIdType.MESH


def split(x):
    hi = x.astype(BF16)
    return hi, (x - hi.astype(F32)).astype(BF16)


def stack(x):
    return jnp.concatenate(split(x), axis=0)


def side(x):
    return jnp.concatenate(split(x), axis=1)


def fold(r):
    n = r.shape[0] // 2
    return (r[:n, :LANES] + r[n:, :LANES]) + r[:n, LANES:]


def times(left, x):
    return fold(jnp.dot(left, side(x), preferred_element_type=F32))


def swap(x):
    return pltpu.roll(x, HALF, 1)


def edge_inner(ref):
    a, b = ref[:, :LANES], ref[:, LANES:]
    low = lax.broadcasted_iota(jnp.int32, a.shape, 1) < HALF
    return jnp.where(low, a, b), swap(jnp.where(low, b, a))


def lane_take(src, lane):
    return jnp.take_along_axis(src, lane, axis=1)


def row_take(ref, row, index):
    got = jnp.zeros(index.shape, jnp.int32)
    width = ref.shape[1]
    for first in range(0, width, LANES):
        size = min(LANES, width - first)
        line = ref[row:row + 1, first:first + size]
        if size < LANES:
            line = jnp.concatenate([line, jnp.zeros((1, LANES - size), jnp.int32)], axis=1)
        tile = jnp.broadcast_to(line, index.shape)
        found = lane_take(tile, index & (LANES - 1))
        got = jnp.where((index >> 7) == first // LANES, found, got)
    return got


def octant_dot(left, x, octant):
    n = x.shape[0]
    whole = stack(x)
    code = jnp.broadcast_to(octant.astype(F32), whole.shape).astype(BF16)
    parts = [jnp.where(code == jnp.asarray(o, BF16), whole, jnp.zeros_like(whole)) for o in range(left.shape[1] // n)]
    high = jnp.concatenate([p[:n] for p in parts], axis=0)
    low = jnp.concatenate([p[n:] for p in parts], axis=0)
    return fold(jnp.dot(left, jnp.concatenate([high, low], axis=1), preferred_element_type=F32))


def slots_of(parent):
    ids = lax.broadcasted_iota(jnp.int32, (LANES, LANES), 0)
    return jnp.where(ids == parent, 1.0, 0.0).astype(BF16)


NT = (((1,), (1,)), ((), ()))


def gather_sum(mapped, slots):
    r = lax.dot_general(stack(mapped), slots, NT, preferred_element_type=F32)
    n = mapped.shape[0]
    return r[:n] + r[n:]


def kernel(
    curves, groups, n_in, *refs
):
    held, done = refs[n_in + 2:2 * n_in + 2], refs[2 * n_in + 2]
    loads = [pltpu.make_async_copy(refs[n], held[n], done.at[n]) for n in range(n_in)]
    for n in (1, 0) + tuple(range(2, n_in)):
        loads[n].start()
    cycle(curves, groups, loads, *held, *refs[n_in:n_in + 2], *refs[2 * n_in + 3:])


def cycle(
    curves, groups, loads,
    rhs_ref, start_ref, level_ref, nbr_ref, kind_ref, own0_ref, own1_ref, own2_ref, own3_ref,
    cnbr_ref, ckind_ref, clevel_ref, stiff_ref, smooth_ref, coup_ref, restr_ref,
    base_ref, step_ref,
    mats, rst, rtst, sst, cnb, ckd, clv, cfield, crhs, crow, cur, res, fix,
    edge_out, from_prev, from_next, part, gpart, hpart,
    esend, erecv, gsend, grecv, hsend, hrecv,
):
    me_c, me_g = lax.axis_index("curve"), lax.axis_index("group")
    me = me_c * groups + me_g
    total = curves * groups
    has_prev, has_next = me > 0, me < total - 1
    prev_id = ((me - 1) // groups, lax.rem(me + groups - 1, groups))
    next_id = ((me + 1) // groups, lax.rem(me + 1, groups))
    kinds_n = coup_ref.shape[0]
    vals = rhs_ref.shape[0]
    per_one = HALF
    per_three = own3_ref.shape[1] // curves
    per_four = cnbr_ref.shape[1] // curves
    ctiles = cfield.shape[1]

    @pl.when(jnp.logical_not(has_prev))
    def _():
        from_prev[...] = jnp.zeros_like(from_prev)

    @pl.when(jnp.logical_not(has_next))
    def _():
        from_next[...] = jnp.zeros_like(from_next)

    barrier = pltpu.get_barrier_semaphore()

    def greet(where):
        pl.semaphore_signal(barrier, inc=1, device_id=where, device_id_type=MESH)

    @pl.when(has_prev)
    def _():
        greet(prev_id)

    @pl.when(has_next)
    def _():
        greet(next_id)

    def over(count, body):
        if count <= 9:
            for off in range(1, count):
                body(off)
        else:
            def step(off, carry):
                body(off)
                return carry
            lax.fori_loop(1, count, step, 0)

    over(groups, lambda off: greet((me_c, lax.rem(me_g + off, groups))))
    over(curves, lambda off: greet((lax.rem(me_c + off, curves), me_g)))
    loads[1].wait()
    start_e, start_i = edge_inner(start_ref)
    edge_out[0] = start_e

    def to_prev(r):
        return pltpu.make_async_remote_copy(
            src_ref=edge_out.at[r], dst_ref=from_next.at[r], send_sem=esend.at[r, 0],
            recv_sem=erecv.at[r, 0], device_id=prev_id, device_id_type=MESH)

    def to_next(r):
        return pltpu.make_async_remote_copy(
            src_ref=edge_out.at[r], dst_ref=from_prev.at[r], send_sem=esend.at[r, 1],
            recv_sem=erecv.at[r, 1], device_id=next_id, device_id_type=MESH)

    def send_edges(r):
        @pl.when(has_prev)
        def _():
            to_prev(r).start()

        @pl.when(has_next)
        def _():
            to_next(r).start()

    def halo(r):
        @pl.when(has_next)
        def _():
            to_prev(r).wait_recv()

        @pl.when(has_prev)
        def _():
            to_next(r).wait_recv()

        low = lax.broadcasted_iota(jnp.int32, (vals, LANES), 1) < HALF
        return jnp.where(low, from_next[r], from_prev[r])

    for n, load in enumerate(loads):
        if n != 1:
            load.wait()

    sst[...] = stack(DAMPING * smooth_ref[...])
    for i in range(mats.shape[2] // LANES):
        two = []
        for t in (2 * i, 2 * i + 1):
            two.append(coup_ref[t] if t < kinds_n else stiff_ref[...] if t == kinds_n else jnp.zeros((vals, vals), F32))
        both = jnp.concatenate(two, axis=1)
        mats[1, :, i * LANES:(i + 1) * LANES] = stack(both)
        mats[0, :, i * LANES:(i + 1) * LANES] = stack(times(sst[...], both))
    for i in range(rst.shape[1] // LANES):
        one, two = restr_ref[2 * i], restr_ref[2 * i + 1]
        cols = slice(i * LANES, (i + 1) * LANES)
        rst[:, cols] = stack(jnp.concatenate([one, two], axis=1))
        rtst[:, cols] = stack(jnp.concatenate([one.T, two.T], axis=1))
    pl.semaphore_wait(barrier, groups + curves - 2 + has_prev.astype(jnp.int32) + has_next.astype(jnp.int32))
    send_edges(0)

    rhs_e, rhs_i = edge_inner(rhs_ref)
    lev_e, lev_i = edge_inner(level_ref)
    scl_e, scl_i = jnp.exp2(lev_e.astype(F32)), jnp.exp2(lev_i.astype(F32))
    gs_e, gs_i = rhs_e * scl_e, rhs_i * scl_i
    nbr_e, nbr_i = edge_inner(nbr_ref)
    kind_e, kind_i = edge_inner(kind_ref)
    lane8 = lax.broadcasted_iota(jnp.int32, (8, LANES), 1)
    at_i = jnp.where(nbr_i != 0, lane8 + HALF + nbr_i, -1000)
    at_e = jnp.where(nbr_e != 0, jnp.where(lane8 < HALF, lane8, lane8 + LANES) + nbr_e, -1000)
    kind_e = jnp.where(nbr_e != 0, kind_e, -1)
    kind_i = jnp.where(nbr_i != 0, kind_i, -1)

    def couple(left, own, kinds, picks):
        slots_n = kinds.shape[0]
        picked = [picks(k) for k in range(slots_n)]
        codes, parts = [], []
        for k in range(slots_n):
            whole = picked[k]
            for other in range(k):
                same = kinds[other:other + 1] == kinds[k:k + 1]
                whole = whole + jnp.where(same, picked[other], 0.0)
            parts.append(stack(whole))
            codes.append(jnp.broadcast_to(kinds[k:k + 1].astype(F32), (2 * vals, LANES)).astype(BF16))
        empty = jnp.zeros_like(parts[0])

        def of_kind(t):
            if t >= kinds_n:
                return stack(own) if t == kinds_n else empty
            acc = empty
            for k in range(slots_n):
                acc = jnp.where(codes[k] == jnp.asarray(t, BF16), parts[k], acc)
            return acc

        totals = [None, None]
        chunk = 4
        for c in range(left.shape[1] // (chunk * vals)):
            found = [of_kind(t) for t in range(c * chunk, (c + 1) * chunk)]
            right = jnp.concatenate([
                jnp.concatenate([f[:vals] for f in found], axis=0),
                jnp.concatenate([f[vals:] for f in found], axis=0)], axis=1)
            r = jnp.dot(left[:, c * chunk * vals:(c + 1) * chunk * vals], right, preferred_element_type=F32)
            totals[c % 2] = r if totals[c % 2] is None else totals[c % 2] + r
        return fold(totals[0] + totals[1])

    def wide(row):
        return jnp.broadcast_to(row, (vals, LANES))

    def places(at):
        inner = (at >= HALF) & (at < HALF + LANES)
        own = (at >= 0) & (at < 2 * LANES)
        lane = at & (LANES - 1)
        return jnp.where(inner, lane ^ HALF, lane), jnp.where(inner, 1, jnp.where(own, 0, 2))

    lane_i, tile_i = places(at_i)
    lane_e, tile_e = places(at_e)

    def inner_image(left, e, i):
        def picks(k):
            lane = wide(lane_i[k:k + 1])
            return jnp.where(wide(tile_i[k:k + 1]) == 1, lane_take(i, lane), lane_take(e, lane))
        return couple(left, i, kind_i, picks)

    def edge_image(left, e, i, h):
        def picks(k):
            lane, tile = wide(lane_e[k:k + 1]), wide(tile_e[k:k + 1])
            got = jnp.where(tile == 0, lane_take(e, lane), lane_take(h, lane))
            return jnp.where(tile == 1, lane_take(i, lane), got)
        return couple(left, e, kind_e, picks)

    fix[0, 0], fix[0, 1] = times(sst[...], gs_e), times(sst[...], gs_i)
    fix[1, 0], fix[1, 1] = rhs_e, rhs_i
    fix[2, 0] = jnp.broadcast_to(1.0 / scl_e, (vals, LANES))
    fix[2, 1] = jnp.broadcast_to(1.0 / scl_i, (vals, LANES))
    cur[0], cur[1] = start_e, start_i

    lane_at = lane8
    own0_e, own0_i = edge_inner(own0_ref)
    at_one = jnp.where(lane_at < per_one, me_g * per_one + lane_at, 0)
    par1, oct1 = row_take(own1_ref, 0, at_one), row_take(own1_ref, 1, at_one)
    at_two = jnp.where(lane_at < own2_ref.shape[1], lane_at, 0)
    par2, oct2 = row_take(own2_ref, 0, at_two), row_take(own2_ref, 1, at_two)
    at_three = jnp.where(lane_at < per_three, me_c * per_three + lane_at, 0)
    par3, oct3 = row_take(own3_ref, 0, at_three), row_take(own3_ref, 1, at_three)

    width = cnbr_ref.shape[1]
    cnb[...] = jnp.full_like(cnb, -1)
    ckd[...] = jnp.full_like(ckd, -1)
    clv[...] = jnp.zeros_like(clv)
    crow[...] = jnp.zeros_like(crow)
    for n in range(ctiles):
        size = min(LANES, width - n * LANES)
        cols = slice(n * LANES, n * LANES + size)
        cnb[n, :, :size] = cnbr_ref[:, cols]
        ckd[n, :, :size] = ckind_ref[:, cols]
        clv[n, :, :size] = jnp.broadcast_to(clevel_ref[:, cols], (8, size))

    def to_group(off):
        return pltpu.make_async_remote_copy(
            src_ref=part, dst_ref=gpart.at[off], send_sem=gsend.at[off], recv_sem=grecv.at[off],
            device_id=(me_c, lax.rem(me_g + off, groups)), device_id_type=MESH)

    def to_curve(off):
        return pltpu.make_async_remote_copy(
            src_ref=hpart.at[me_c], dst_ref=hpart.at[me_c], send_sem=hsend.at[off], recv_sem=hrecv.at[off],
            device_id=(lax.rem(me_c + off, curves), me_g), device_id_type=MESH)

    def from_curve(off):
        who = lax.rem(me_c + curves - off, curves)
        return pltpu.make_async_remote_copy(
            src_ref=hpart.at[who], dst_ref=hpart.at[who], send_sem=hsend.at[off], recv_sem=hrecv.at[off],
            device_id=(lax.rem(me_c + off, curves), me_g), device_id_type=MESH)

    def middle():
        one = (gather_sum(octant_dot(rst[...], res[0], own0_e[1:2]), slots_of(own0_e[0:1]))
               + gather_sum(octant_dot(rst[...], res[1], own0_i[1:2]), slots_of(own0_i[0:1])))
        two = gather_sum(octant_dot(rst[...], one, oct1[0:1]), slots_of(par1[0:1]))
        three = gather_sum(octant_dot(rst[...], two, oct2[0:1]), slots_of(par2[0:1]))
        mapped = octant_dot(rst[...], three, oct3[0:1])
        ids = lax.broadcasted_iota(jnp.int32, (8, LANES), 0)
        slots = jnp.where(ids == par3[0:1], 1.0, 0.0).astype(BF16)
        hi, lo = split(mapped)
        zeros = jnp.zeros_like(hi)
        part[...] = (lax.dot_general(slots, jnp.concatenate([hi, zeros], axis=0), NT, preferred_element_type=F32)
                     + lax.dot_general(slots, jnp.concatenate([lo, zeros], axis=0), NT, preferred_element_type=F32))

        over(groups, lambda off: to_group(off).start())
        over(groups, lambda off: to_group(off).wait_recv())
        mine = part[...]
        for off in range(1, groups):
            mine = mine + gpart[off]
        hpart[me_c] = mine
        over(curves, lambda off: to_curve(off).start())
        over(curves, lambda off: from_curve(off).wait_recv())

        for m in range(curves):
            crow[m * per_four:(m + 1) * per_four, :] = hpart[m, :per_four, :]
        for n in range(ctiles):
            block = crow[n * LANES:(n + 1) * LANES, :].T[:vals]
            crhs[n] = times(sst[...], block * jnp.exp2(clv[n, 0:1].astype(F32)))
            cfield[0, n] = crhs[n]

        def coarse_step(s, carry):
            sweep, n = s // ctiles, lax.rem(s, ctiles)
            old = lax.rem(sweep, 2)
            at_c = cnb[n]
            kind_c = jnp.where(at_c >= 0, ckd[n], -1)
            field = [cfield[old, m] for m in range(ctiles)]
            own = cfield[old, n]

            def picks(k):
                at = wide(at_c[k:k + 1])
                lane = at & (LANES - 1)
                got = lane_take(field[0], lane)
                for m in range(1, ctiles):
                    got = jnp.where((at >> 7) == m, lane_take(field[m], lane), got)
                return got

            cfield[1 - old, n] = own + (crhs[n] - couple(mats.at[0], own, kind_c, picks))
            return carry

        lax.fori_loop(0, (COARSE_SWEEPS - 1) * ctiles, coarse_step, 0)
        field = [cfield[(COARSE_SWEEPS - 1) % 2, m] for m in range(ctiles)]

        at = wide(jnp.where(lane_at < per_three, me_c * per_four + par3, 0)[0:1])
        back = lane_take(field[0], at & (LANES - 1))
        for s in range(1, ctiles):
            back = jnp.where((at >> 7) == s, lane_take(field[s], at & (LANES - 1)), back)
        back = octant_dot(rtst[...], back, oct3[0:1])
        back = octant_dot(rtst[...], lane_take(back, wide(par2[0:1])), oct2[0:1])
        back = octant_dot(rtst[...], lane_take(back, wide(par1[0:1])), oct1[0:1])
        e = cur[0] + octant_dot(rtst[...], lane_take(back, wide(own0_e[0:1])), own0_e[1:2])
        edge_out[3] = e
        cur[0] = e
        send_edges(3)
        cur[1] = cur[1] + octant_dot(rtst[...], lane_take(back, wide(own0_i[0:1])), own0_i[1:2])

    def sweep(r, carry):
        @pl.when(r == 3)
        def _():
            middle()

        left = mats.at[(r == 2).astype(jnp.int32)]
        inner = inner_image(left, cur[0], cur[1])
        edge = edge_image(left, cur[0], cur[1], halo(r))

        @pl.when(r == 2)
        def _():
            res[0] = fix[1, 0] - edge * fix[2, 0]
            res[1] = fix[1, 1] - inner * fix[2, 1]

        @pl.when(r < 2)
        def _():
            new = cur[0] + (fix[0, 0] - edge)
            cur[0] = new
            cur[1] = cur[1] + (fix[0, 1] - inner)
            edge_out[r + 1] = new
            send_edges(r + 1)

        @pl.when(r == 3)
        def _():
            low = lax.broadcasted_iota(jnp.int32, (vals, LANES), 1) < HALF
            for ref, e, i in ((base_ref, cur[0], cur[1]), (step_ref, fix[0, 0] - edge, fix[0, 1] - inner)):
                turned = swap(i)
                ref[:, :LANES] = jnp.where(low, e, turned)
                ref[:, LANES:] = jnp.where(low, turned, e)

        return carry

    lax.fori_loop(0, 4, sweep, 0)

    over(groups, lambda off: to_group(off).wait_send())
    over(curves, lambda off: to_curve(off).wait_send())

    @pl.when(has_prev)
    def _():
        for r in range(4):
            to_prev(r).wait_send()

    @pl.when(has_next)
    def _():
        for r in range(4):
            to_next(r).wait_send()


def solution(mesh):
    curves, groups = mesh.shape["curve"], mesh.shape["group"]

    def shards(*args):
        args = list(args)
        args[2] = args[2].reshape(1, -1)
        args[11] = args[11].reshape(1, -1)
        rhs, coup, restr = args[0], args[14], args[15]
        vals, blocks = rhs.shape
        kinds = coup.shape[0] + 1
        depth = -(-kinds // 4) * 4 * vals
        cw = -(-args[9].shape[1] // LANES) * LANES
        rdepth = restr.shape[0] * vals
        assert blocks == 2 * LANES and vals == HALF
        vm = pltpu.VMEM
        base, step = pl.pallas_call(
            functools.partial(kernel, curves, groups, len(args)),
            out_shape=[jax.ShapeDtypeStruct(rhs.shape, F32)] * 2,
            in_specs=[pl.BlockSpec(memory_space=pltpu.HBM)] * len(args),
            out_specs=[pl.BlockSpec(memory_space=pltpu.VMEM)] * 2,
            scratch_shapes=[vm(a.shape, a.dtype) for a in args] + [
                pltpu.SemaphoreType.DMA((len(args),)),
                vm((2, 2 * vals, depth), BF16),
                vm((2 * vals, rdepth), BF16),
                vm((2 * vals, rdepth), BF16),
                vm((2 * vals, vals), BF16),
                vm((cw // LANES, 8, LANES), jnp.int32),
                vm((cw // LANES, 8, LANES), jnp.int32),
                vm((cw // LANES, 8, LANES), jnp.int32),
                vm((2, cw // LANES, vals, LANES), F32),
                vm((cw // LANES, vals, LANES), F32),
                vm((cw, LANES), F32),
                vm((2, vals, LANES), F32),
                vm((2, vals, LANES), F32),
                vm((3, 2, vals, LANES), F32),
                vm((4, vals, LANES), F32),
                vm((4, vals, LANES), F32),
                vm((4, vals, LANES), F32),
                vm((8, LANES), F32),
                vm((groups, 8, LANES), F32),
                vm((curves, 8, LANES), F32),
                pltpu.SemaphoreType.DMA((4, 2)),
                pltpu.SemaphoreType.DMA((4, 2)),
                pltpu.SemaphoreType.DMA((groups,)),
                pltpu.SemaphoreType.DMA((groups,)),
                pltpu.SemaphoreType.DMA((curves,)),
                pltpu.SemaphoreType.DMA((curves,)),
            ],
            compiler_params=pltpu.CompilerParams(
                collective_id=0, has_side_effects=True, vmem_limit_bytes=60 * 2**20
            ),
        )(*args)
        return base + step

    fine, part, all_ = P(None, ("curve", "group")), P(None, "curve"), P()
    return jax.shard_map(
        shards,
        mesh=mesh,
        in_specs=(fine, fine, P(("curve", "group")), fine, fine, fine, part, part) + (all_,) * 8,
        out_specs=fine,
        check_vma=False,
    )
```

```python
import functools

import jax
import jax.numpy as jnp
from jax import lax
from jax.experimental import pallas as pl
from jax.experimental.pallas import tpu as pltpu
from jax.sharding import PartitionSpec as P

DAMPING = 0.7
COARSE_SWEEPS = 3
LANES = 128
HALF = 64
F32, BF16 = jnp.float32, jnp.bfloat16
MESH = pl.DeviceIdType.MESH


def split(x):
    hi = x.astype(BF16)
    return hi, (x - hi.astype(F32)).astype(BF16)


def stack(x):
    return jnp.concatenate(split(x), axis=0)


def side(x):
    return jnp.concatenate(split(x), axis=1)


def fold(r):
    n = r.shape[0] // 2
    return (r[:n, :LANES] + r[n:, :LANES]) + r[:n, LANES:]


def times(left, x):
    return fold(jnp.dot(left, side(x), preferred_element_type=F32))


def swap(x):
    return pltpu.roll(x, HALF, 1)


def edge_inner(ref):
    a, b = ref[:, :LANES], ref[:, LANES:]
    low = lax.broadcasted_iota(jnp.int32, a.shape, 1) < HALF
    return jnp.where(low, a, b), swap(jnp.where(low, b, a))


def lane_take(src, lane):
    return jnp.take_along_axis(src, lane, axis=1)


def row_take(ref, row, index):
    got = jnp.zeros(index.shape, jnp.int32)
    width = ref.shape[1]
    for first in range(0, width, LANES):
        size = min(LANES, width - first)
        line = ref[row:row + 1, first:first + size]
        if size < LANES:
            line = jnp.concatenate([line, jnp.zeros((1, LANES - size), jnp.int32)], axis=1)
        tile = jnp.broadcast_to(line, index.shape)
        found = lane_take(tile, index & (LANES - 1))
        got = jnp.where((index >> 7) == first // LANES, found, got)
    return got


def octant_dot(left, x, octant):
    n = x.shape[0]
    whole = stack(x)
    code = jnp.broadcast_to(octant.astype(F32), whole.shape).astype(BF16)
    parts = [jnp.where(code == jnp.asarray(o, BF16), whole, jnp.zeros_like(whole)) for o in range(left.shape[1] // n)]
    high = jnp.concatenate([p[:n] for p in parts], axis=0)
    low = jnp.concatenate([p[n:] for p in parts], axis=0)
    return fold(jnp.dot(left, jnp.concatenate([high, low], axis=1), preferred_element_type=F32))


def slots_of(parent):
    ids = lax.broadcasted_iota(jnp.int32, (LANES, LANES), 0)
    return jnp.where(ids == parent, 1.0, 0.0).astype(BF16)


NT = (((1,), (1,)), ((), ()))


def gather_sum(mapped, slots):
    r = lax.dot_general(stack(mapped), slots, NT, preferred_element_type=F32)
    n = mapped.shape[0]
    return r[:n] + r[n:]


def kernel(
    curves, groups, n_in, *refs
):
    held, done = refs[n_in + 2:2 * n_in + 2], refs[2 * n_in + 2]
    loads = [pltpu.make_async_copy(refs[n], held[n], done.at[n]) for n in range(n_in)]
    for n in (1, 0) + tuple(range(2, n_in)):
        loads[n].start()
    cycle(curves, groups, loads, *held, *refs[n_in:n_in + 2], *refs[2 * n_in + 3:])


def cycle(
    curves, groups, loads,
    rhs_ref, start_ref, level_ref, nbr_ref, kind_ref, own0_ref, own1_ref, own2_ref, own3_ref,
    cnbr_ref, ckind_ref, clevel_ref, stiff_ref, smooth_ref, coup_ref, restr_ref,
    base_ref, step_ref,
    mats, rst, rtst, sst, cnb, ckd, clv, cfield, crhs, crow, cur, res, fix,
    edge_out, from_prev, from_next, part, gpart, hpart,
    esend, erecv, gsend, grecv, hsend, hrecv,
):
    me_c, me_g = lax.axis_index("curve"), lax.axis_index("group")
    me = me_c * groups + me_g
    total = curves * groups
    has_prev, has_next = me > 0, me < total - 1
    prev_id = ((me - 1) // groups, lax.rem(me + groups - 1, groups))
    next_id = ((me + 1) // groups, lax.rem(me + 1, groups))
    kinds_n = coup_ref.shape[0]
    vals = rhs_ref.shape[0]
    per_one = HALF
    per_three = own3_ref.shape[1] // curves
    per_four = cnbr_ref.shape[1] // curves
    ctiles = cfield.shape[1]

    @pl.when(jnp.logical_not(has_prev))
    def _():
        from_prev[...] = jnp.zeros_like(from_prev)

    @pl.when(jnp.logical_not(has_next))
    def _():
        from_next[...] = jnp.zeros_like(from_next)

    barrier = pltpu.get_barrier_semaphore()

    def greet(where):
        pl.semaphore_signal(barrier, inc=1, device_id=where, device_id_type=MESH)

    @pl.when(has_prev)
    def _():
        greet(prev_id)

    @pl.when(has_next)
    def _():
        greet(next_id)

    def over(count, body):
        if count <= 9:
            for off in range(1, count):
                body(off)
        else:
            def step(off, carry):
                body(off)
                return carry
            lax.fori_loop(1, count, step, 0)

    over(groups, lambda off: greet((me_c, lax.rem(me_g + off, groups))))
    over(curves, lambda off: greet((lax.rem(me_c + off, curves), me_g)))
    loads[1].wait()
    start_e, start_i = edge_inner(start_ref)
    edge_out[0] = start_e

    def to_prev(r):
        return pltpu.make_async_remote_copy(
            src_ref=edge_out.at[r], dst_ref=from_next.at[r], send_sem=esend.at[r, 0],
            recv_sem=erecv.at[r, 0], device_id=prev_id, device_id_type=MESH)

    def to_next(r):
        return pltpu.make_async_remote_copy(
            src_ref=edge_out.at[r], dst_ref=from_prev.at[r], send_sem=esend.at[r, 1],
            recv_sem=erecv.at[r, 1], device_id=next_id, device_id_type=MESH)

    def send_edges(r):
        @pl.when(has_prev)
        def _():
            to_prev(r).start()

        @pl.when(has_next)
        def _():
            to_next(r).start()

    def halo(r):
        @pl.when(has_next)
        def _():
            to_prev(r).wait_recv()

        @pl.when(has_prev)
        def _():
            to_next(r).wait_recv()

        low = lax.broadcasted_iota(jnp.int32, (vals, LANES), 1) < HALF
        return jnp.where(low, from_next[r], from_prev[r])

    for n, load in enumerate(loads):
        if n != 1:
            load.wait()

    sst[...] = stack(DAMPING * smooth_ref[...])
    for i in range(mats.shape[2] // LANES):
        two = []
        for t in (2 * i, 2 * i + 1):
            two.append(coup_ref[t] if t < kinds_n else stiff_ref[...] if t == kinds_n else jnp.zeros((vals, vals), F32))
        both = jnp.concatenate(two, axis=1)
        mats[1, :, i * LANES:(i + 1) * LANES] = stack(both)
        mats[0, :, i * LANES:(i + 1) * LANES] = stack(times(sst[...], both))
    for i in range(rst.shape[1] // LANES):
        one, two = restr_ref[2 * i], restr_ref[2 * i + 1]
        cols = slice(i * LANES, (i + 1) * LANES)
        rst[:, cols] = stack(jnp.concatenate([one, two], axis=1))
        rtst[:, cols] = stack(jnp.concatenate([one.T, two.T], axis=1))
    pl.semaphore_wait(barrier, groups + curves - 2 + has_prev.astype(jnp.int32) + has_next.astype(jnp.int32))
    send_edges(0)

    rhs_e, rhs_i = edge_inner(rhs_ref)
    lev_e, lev_i = edge_inner(level_ref)
    scl_e, scl_i = jnp.exp2(lev_e.astype(F32)), jnp.exp2(lev_i.astype(F32))
    gs_e, gs_i = rhs_e * scl_e, rhs_i * scl_i
    nbr_e, nbr_i = edge_inner(nbr_ref)
    kind_e, kind_i = edge_inner(kind_ref)
    lane8 = lax.broadcasted_iota(jnp.int32, (8, LANES), 1)
    at_i = jnp.where(nbr_i != 0, lane8 + HALF + nbr_i, -1000)
    at_e = jnp.where(nbr_e != 0, jnp.where(lane8 < HALF, lane8, lane8 + LANES) + nbr_e, -1000)
    kind_e = jnp.where(nbr_e != 0, kind_e, -1)
    kind_i = jnp.where(nbr_i != 0, kind_i, -1)

    def couple(left, own, kinds, picks):
        slots_n = kinds.shape[0]
        picked = [picks(k) for k in range(slots_n)]
        codes, parts = [], []
        for k in range(slots_n):
            whole = picked[k]
            for other in range(k):
                same = kinds[other:other + 1] == kinds[k:k + 1]
                whole = whole + jnp.where(same, picked[other], 0.0)
            parts.append(stack(whole))
            codes.append(jnp.broadcast_to(kinds[k:k + 1].astype(F32), (2 * vals, LANES)).astype(BF16))
        empty = jnp.zeros_like(parts[0])

        def of_kind(t):
            if t >= kinds_n:
                return stack(own) if t == kinds_n else empty
            acc = empty
            for k in range(slots_n):
                acc = jnp.where(codes[k] == jnp.asarray(t, BF16), parts[k], acc)
            return acc

        totals = [None, None]
        chunk = 4
        for c in range(left.shape[1] // (chunk * vals)):
            found = [of_kind(t) for t in range(c * chunk, (c + 1) * chunk)]
            right = jnp.concatenate([
                jnp.concatenate([f[:vals] for f in found], axis=0),
                jnp.concatenate([f[vals:] for f in found], axis=0)], axis=1)
            r = jnp.dot(left[:, c * chunk * vals:(c + 1) * chunk * vals], right, preferred_element_type=F32)
            totals[c % 2] = r if totals[c % 2] is None else totals[c % 2] + r
        return fold(totals[0] + totals[1])

    def wide(row):
        return jnp.broadcast_to(row, (vals, LANES))

    def places(at):
        inner = (at >= HALF) & (at < HALF + LANES)
        own = (at >= 0) & (at < 2 * LANES)
        lane = at & (LANES - 1)
        return jnp.where(inner, lane ^ HALF, lane), jnp.where(inner, 1, jnp.where(own, 0, 2))

    lane_i, tile_i = places(at_i)
    lane_e, tile_e = places(at_e)

    def inner_image(left, e, i):
        def picks(k):
            lane = wide(lane_i[k:k + 1])
            return jnp.where(wide(tile_i[k:k + 1]) == 1, lane_take(i, lane), lane_take(e, lane))
        return couple(left, i, kind_i, picks)

    def edge_image(left, e, i, h):
        def picks(k):
            lane, tile = wide(lane_e[k:k + 1]), wide(tile_e[k:k + 1])
            got = jnp.where(tile == 0, lane_take(e, lane), lane_take(h, lane))
            return jnp.where(tile == 1, lane_take(i, lane), got)
        return couple(left, e, kind_e, picks)

    fix[0, 0], fix[0, 1] = times(sst[...], gs_e), times(sst[...], gs_i)
    fix[1, 0], fix[1, 1] = rhs_e, rhs_i
    fix[2, 0] = jnp.broadcast_to(1.0 / scl_e, (vals, LANES))
    fix[2, 1] = jnp.broadcast_to(1.0 / scl_i, (vals, LANES))
    cur[0], cur[1] = start_e, start_i

    lane_at = lane8
    own0_e, own0_i = edge_inner(own0_ref)
    at_one = jnp.where(lane_at < per_one, me_g * per_one + lane_at, 0)
    par1, oct1 = row_take(own1_ref, 0, at_one), row_take(own1_ref, 1, at_one)
    at_two = jnp.where(lane_at < own2_ref.shape[1], lane_at, 0)
    par2, oct2 = row_take(own2_ref, 0, at_two), row_take(own2_ref, 1, at_two)
    at_three = jnp.where(lane_at < per_three, me_c * per_three + lane_at, 0)
    par3, oct3 = row_take(own3_ref, 0, at_three), row_take(own3_ref, 1, at_three)

    slots_all, width = cnbr_ref.shape
    rep = LANES // width if width < LANES and LANES % width == 0 else 1
    rep = rep if slots_all % rep == 0 else 1
    rows_n = slots_all // rep
    cnb[...] = jnp.full_like(cnb, -1)
    ckd[...] = jnp.full_like(ckd, -1)
    clv[...] = jnp.zeros_like(clv)
    crow[...] = jnp.zeros_like(crow)
    for n in range(ctiles):
        size = min(LANES, width - n * LANES)
        cols = slice(n * LANES, n * LANES + size)
        for g in range(rep):
            rows, place = slice(g * rows_n, (g + 1) * rows_n), slice(g * size, (g + 1) * size)
            cnb[n, :rows_n, place] = cnbr_ref[rows, cols]
            ckd[n, :rows_n, place] = ckind_ref[rows, cols]
        clv[n, :, :size] = jnp.broadcast_to(clevel_ref[:, cols], (8, size))

    def to_group(off):
        return pltpu.make_async_remote_copy(
            src_ref=part, dst_ref=gpart.at[off], send_sem=gsend.at[off], recv_sem=grecv.at[off],
            device_id=(me_c, lax.rem(me_g + off, groups)), device_id_type=MESH)

    def to_curve(off):
        return pltpu.make_async_remote_copy(
            src_ref=hpart.at[me_c], dst_ref=hpart.at[me_c], send_sem=hsend.at[off], recv_sem=hrecv.at[off],
            device_id=(lax.rem(me_c + off, curves), me_g), device_id_type=MESH)

    def from_curve(off):
        who = lax.rem(me_c + curves - off, curves)
        return pltpu.make_async_remote_copy(
            src_ref=hpart.at[who], dst_ref=hpart.at[who], send_sem=hsend.at[off], recv_sem=hrecv.at[off],
            device_id=(lax.rem(me_c + off, curves), me_g), device_id_type=MESH)

    def middle():
        one = (gather_sum(octant_dot(rst[...], res[0], own0_e[1:2]), slots_of(own0_e[0:1]))
               + gather_sum(octant_dot(rst[...], res[1], own0_i[1:2]), slots_of(own0_i[0:1])))
        two = gather_sum(octant_dot(rst[...], one, oct1[0:1]), slots_of(par1[0:1]))
        three = gather_sum(octant_dot(rst[...], two, oct2[0:1]), slots_of(par2[0:1]))
        mapped = octant_dot(rst[...], three, oct3[0:1])
        ids = lax.broadcasted_iota(jnp.int32, (8, LANES), 0)
        slots = jnp.where(ids == par3[0:1], 1.0, 0.0).astype(BF16)
        hi, lo = split(mapped)
        zeros = jnp.zeros_like(hi)
        sums = (lax.dot_general(slots, jnp.concatenate([hi, zeros], axis=0), NT, preferred_element_type=F32)
                     + lax.dot_general(slots, jnp.concatenate([lo, zeros], axis=0), NT, preferred_element_type=F32))

        part[...] = sums[:per_four]
        over(groups, lambda off: to_group(off).start())
        over(groups, lambda off: to_group(off).wait_recv())
        mine = part[...]
        for off in range(1, groups):
            mine = mine + gpart[off]
        hpart[me_c] = mine
        over(curves, lambda off: to_curve(off).start())
        over(curves, lambda off: from_curve(off).wait_recv())

        for m in range(curves):
            crow[m * per_four:(m + 1) * per_four, :] = hpart[m]
        for n in range(ctiles):
            block = crow[n * LANES:(n + 1) * LANES, :].T[:vals]
            crhs[n] = times(sst[...], block * jnp.exp2(clv[n, 0:1].astype(F32)))
            cfield[0, n] = crhs[n]

        def coarse_step(s, carry):
            sweep, n = s // ctiles, lax.rem(s, ctiles)
            old = lax.rem(sweep, 2)
            at_c = cnb[n, :rows_n]
            kind_c = jnp.where(at_c >= 0, ckd[n, :rows_n], -1)
            field = [cfield[old, m] for m in range(ctiles)]
            own = cfield[old, n]

            def picks(k):
                at = wide(at_c[k:k + 1])
                lane = at & (LANES - 1)
                got = lane_take(field[0], lane)
                for m in range(1, ctiles):
                    got = jnp.where((at >> 7) == m, lane_take(field[m], lane), got)
                return got

            once = own
            if rep > 1:
                once = jnp.where(lax.broadcasted_iota(jnp.int32, own.shape, 1) < width, own, 0.0)
            image = couple(mats.at[0], once, kind_c, picks)
            total = image
            for g in range(1, rep):
                total = total + pltpu.roll(image, g * width, 1)
            cfield[1 - old, n] = own + (crhs[n] - total)
            return carry

        lax.fori_loop(0, (COARSE_SWEEPS - 1) * ctiles, coarse_step, 0)
        field = [cfield[(COARSE_SWEEPS - 1) % 2, m] for m in range(ctiles)]

        at = wide(jnp.where(lane_at < per_three, me_c * per_four + par3, 0)[0:1])
        back = lane_take(field[0], at & (LANES - 1))
        for s in range(1, ctiles):
            back = jnp.where((at >> 7) == s, lane_take(field[s], at & (LANES - 1)), back)
        back = octant_dot(rtst[...], back, oct3[0:1])
        back = octant_dot(rtst[...], lane_take(back, wide(par2[0:1])), oct2[0:1])
        back = octant_dot(rtst[...], lane_take(back, wide(par1[0:1])), oct1[0:1])
        e = cur[0] + octant_dot(rtst[...], lane_take(back, wide(own0_e[0:1])), own0_e[1:2])
        edge_out[3] = e
        cur[0] = e
        send_edges(3)
        cur[1] = cur[1] + octant_dot(rtst[...], lane_take(back, wide(own0_i[0:1])), own0_i[1:2])

    def sweep(r, carry):
        @pl.when(r == 3)
        def _():
            middle()

        left = mats.at[(r == 2).astype(jnp.int32)]
        inner = inner_image(left, cur[0], cur[1])
        edge = edge_image(left, cur[0], cur[1], halo(r))

        @pl.when(r == 2)
        def _():
            res[0] = fix[1, 0] - edge * fix[2, 0]
            res[1] = fix[1, 1] - inner * fix[2, 1]

        @pl.when(r < 2)
        def _():
            new = cur[0] + (fix[0, 0] - edge)
            cur[0] = new
            cur[1] = cur[1] + (fix[0, 1] - inner)
            edge_out[r + 1] = new
            send_edges(r + 1)

        @pl.when(r == 3)
        def _():
            low = lax.broadcasted_iota(jnp.int32, (vals, LANES), 1) < HALF
            for ref, e, i in ((base_ref, cur[0], cur[1]), (step_ref, fix[0, 0] - edge, fix[0, 1] - inner)):
                turned = swap(i)
                ref[:, :LANES] = jnp.where(low, e, turned)
                ref[:, LANES:] = jnp.where(low, turned, e)

        return carry

    lax.fori_loop(0, 4, sweep, 0)

    over(groups, lambda off: to_group(off).wait_send())
    over(curves, lambda off: to_curve(off).wait_send())

    @pl.when(has_prev)
    def _():
        for r in range(4):
            to_prev(r).wait_send()

    @pl.when(has_next)
    def _():
        for r in range(4):
            to_next(r).wait_send()


def solution(mesh):
    curves, groups = mesh.shape["curve"], mesh.shape["group"]

    def shards(*args):
        args = list(args)
        args[2] = args[2].reshape(1, -1)
        args[11] = args[11].reshape(1, -1)
        rhs, coup, restr = args[0], args[14], args[15]
        vals, blocks = rhs.shape
        kinds = coup.shape[0] + 1
        depth = -(-kinds // 4) * 4 * vals
        cw = -(-args[9].shape[1] // LANES) * LANES
        four = args[9].shape[1] // curves
        rdepth = restr.shape[0] * vals
        assert blocks == 2 * LANES and vals == HALF
        vm = pltpu.VMEM
        base, step = pl.pallas_call(
            functools.partial(kernel, curves, groups, len(args)),
            out_shape=[jax.ShapeDtypeStruct(rhs.shape, F32)] * 2,
            in_specs=[pl.BlockSpec(memory_space=pltpu.HBM)] * len(args),
            out_specs=[pl.BlockSpec(memory_space=pltpu.VMEM)] * 2,
            scratch_shapes=[vm(a.shape, a.dtype) for a in args] + [
                pltpu.SemaphoreType.DMA((len(args),)),
                vm((2, 2 * vals, depth), BF16),
                vm((2 * vals, rdepth), BF16),
                vm((2 * vals, rdepth), BF16),
                vm((2 * vals, vals), BF16),
                vm((cw // LANES, 8, LANES), jnp.int32),
                vm((cw // LANES, 8, LANES), jnp.int32),
                vm((cw // LANES, 8, LANES), jnp.int32),
                vm((2, cw // LANES, vals, LANES), F32),
                vm((cw // LANES, vals, LANES), F32),
                vm((cw, LANES), F32),
                vm((2, vals, LANES), F32),
                vm((2, vals, LANES), F32),
                vm((3, 2, vals, LANES), F32),
                vm((4, vals, LANES), F32),
                vm((4, vals, LANES), F32),
                vm((4, vals, LANES), F32),
                vm((four, LANES), F32),
                vm((groups, four, LANES), F32),
                vm((curves, four, LANES), F32),
                pltpu.SemaphoreType.DMA((4, 2)),
                pltpu.SemaphoreType.DMA((4, 2)),
                pltpu.SemaphoreType.DMA((groups,)),
                pltpu.SemaphoreType.DMA((groups,)),
                pltpu.SemaphoreType.DMA((curves,)),
                pltpu.SemaphoreType.DMA((curves,)),
            ],
            compiler_params=pltpu.CompilerParams(
                collective_id=0, has_side_effects=True, vmem_limit_bytes=60 * 2**20
            ),
        )(*args)
        return base + step

    fine, part, all_ = P(None, ("curve", "group")), P(None, "curve"), P()
    return jax.shard_map(
        shards,
        mesh=mesh,
        in_specs=(fine, fine, P(("curve", "group")), fine, fine, fine, part, part) + (all_,) * 8,
        out_specs=fine,
        check_vma=False,
    )
```

```python
import functools

import jax
import jax.numpy as jnp
from jax import lax
from jax.experimental import pallas as pl
from jax.experimental.pallas import tpu as pltpu
from jax.sharding import PartitionSpec as P

DAMPING = 0.7
COARSE_SWEEPS = 3
LANES = 128
HALF = 64
F32, BF16 = jnp.float32, jnp.bfloat16
MESH = pl.DeviceIdType.MESH


def split(x):
    hi = x.astype(BF16)
    return hi, (x - hi.astype(F32)).astype(BF16)


def stack(x):
    return jnp.concatenate(split(x), axis=0)


def side(x):
    return jnp.concatenate(split(x), axis=1)


def fold(r):
    n = r.shape[0] // 2
    return (r[:n, :LANES] + r[n:, :LANES]) + r[:n, LANES:]


def times(left, x):
    return fold(jnp.dot(left, side(x), preferred_element_type=F32))


def swap(x):
    return pltpu.roll(x, HALF, 1)


def edge_inner(ref):
    a, b = ref[:, :LANES], ref[:, LANES:]
    low = lax.broadcasted_iota(jnp.int32, a.shape, 1) < HALF
    return jnp.where(low, a, b), swap(jnp.where(low, b, a))


def lane_take(src, lane):
    return jnp.take_along_axis(src, lane, axis=1)


def row_take(ref, row, index):
    got = jnp.zeros(index.shape, jnp.int32)
    width = ref.shape[1]
    for first in range(0, width, LANES):
        size = min(LANES, width - first)
        line = ref[row:row + 1, first:first + size]
        if size < LANES:
            line = jnp.concatenate([line, jnp.zeros((1, LANES - size), jnp.int32)], axis=1)
        tile = jnp.broadcast_to(line, index.shape)
        found = lane_take(tile, index & (LANES - 1))
        got = jnp.where((index >> 7) == first // LANES, found, got)
    return got


def octant_dot(left, x, octant):
    n = x.shape[0]
    whole = stack(x)
    code = jnp.broadcast_to(octant.astype(F32), whole.shape).astype(BF16)
    parts = [jnp.where(code == jnp.asarray(o, BF16), whole, jnp.zeros_like(whole)) for o in range(left.shape[1] // n)]
    high = jnp.concatenate([p[:n] for p in parts], axis=0)
    low = jnp.concatenate([p[n:] for p in parts], axis=0)
    return fold(jnp.dot(left, jnp.concatenate([high, low], axis=1), preferred_element_type=F32))


def slots_of(parent):
    ids = lax.broadcasted_iota(jnp.int32, (LANES, LANES), 0)
    return jnp.where(ids == parent, 1.0, 0.0).astype(BF16)


NT = (((1,), (1,)), ((), ()))


def gather_sum(mapped, slots):
    r = lax.dot_general(stack(mapped), slots, NT, preferred_element_type=F32)
    n = mapped.shape[0]
    return r[:n] + r[n:]


def kernel(
    curves, groups, n_in, *refs
):
    held, done = refs[n_in + 2:2 * n_in + 2], refs[2 * n_in + 2]
    loads = [pltpu.make_async_copy(refs[n], held[n], done.at[n]) for n in range(n_in)]
    for n in (1, 0) + tuple(range(2, n_in)):
        loads[n].start()
    cycle(curves, groups, loads, *held, *refs[n_in:n_in + 2], *refs[2 * n_in + 3:])


def cycle(
    curves, groups, loads,
    rhs_ref, start_ref, level_ref, nbr_ref, kind_ref, own0_ref, own1_ref, own2_ref, own3_ref,
    cnbr_ref, ckind_ref, clevel_ref, stiff_ref, smooth_ref, coup_ref, restr_ref,
    base_ref, step_ref,
    mats, rst, rtst, sst, cnb, ckd, clv, cfield, crhs, crow, cur, res, fix,
    edge_out, from_prev, from_next, part, gpart, hpart,
    esend, erecv, gsend, grecv, hsend, hrecv,
):
    me_c, me_g = lax.axis_index("curve"), lax.axis_index("group")
    me = me_c * groups + me_g
    total = curves * groups
    has_prev, has_next = me > 0, me < total - 1
    prev_id = ((me - 1) // groups, lax.rem(me + groups - 1, groups))
    next_id = ((me + 1) // groups, lax.rem(me + 1, groups))
    kinds_n = coup_ref.shape[0]
    vals = rhs_ref.shape[0]
    per_one = HALF
    per_three = own3_ref.shape[1] // curves
    per_four = cnbr_ref.shape[1] // curves
    ctiles = cfield.shape[1]

    half = vals // 2
    low_half = lax.broadcasted_iota(jnp.int32, (half, LANES), 1) < HALF

    def pack_edges(r, e):
        turned = swap(e[half:])
        edge_out[r, 0] = jnp.where(low_half, e[:half], turned)
        edge_out[r, 1] = jnp.where(low_half, turned, e[:half])

    @pl.when(jnp.logical_not(has_prev))
    def _():
        from_prev[...] = jnp.zeros_like(from_prev)

    @pl.when(jnp.logical_not(has_next))
    def _():
        from_next[...] = jnp.zeros_like(from_next)

    barrier = pltpu.get_barrier_semaphore()

    def greet(where):
        pl.semaphore_signal(barrier, inc=1, device_id=where, device_id_type=MESH)

    @pl.when(has_prev)
    def _():
        greet(prev_id)

    @pl.when(has_next)
    def _():
        greet(next_id)

    def over(count, body):
        if count <= 9:
            for off in range(1, count):
                body(off)
        else:
            def step(off, carry):
                body(off)
                return carry
            lax.fori_loop(1, count, step, 0)

    over(groups, lambda off: greet((me_c, lax.rem(me_g + off, groups))))
    over(curves, lambda off: greet((lax.rem(me_c + off, curves), me_g)))
    loads[1].wait()
    start_e, start_i = edge_inner(start_ref)
    pack_edges(0, start_e)

    def to_prev(r):
        return pltpu.make_async_remote_copy(
            src_ref=edge_out.at[r, 0], dst_ref=from_next.at[r], send_sem=esend.at[r, 0],
            recv_sem=erecv.at[r, 0], device_id=prev_id, device_id_type=MESH)

    def to_next(r):
        return pltpu.make_async_remote_copy(
            src_ref=edge_out.at[r, 1], dst_ref=from_prev.at[r], send_sem=esend.at[r, 1],
            recv_sem=erecv.at[r, 1], device_id=next_id, device_id_type=MESH)

    def send_edges(r):
        @pl.when(has_prev)
        def _():
            to_prev(r).start()

        @pl.when(has_next)
        def _():
            to_next(r).start()

    def halo(r):
        @pl.when(has_next)
        def _():
            to_prev(r).wait_recv()

        @pl.when(has_prev)
        def _():
            to_next(r).wait_recv()

        after, before = from_next[r], from_prev[r]
        return jnp.concatenate(
            [jnp.where(low_half, after, before), swap(jnp.where(low_half, before, after))], axis=0)

    for n, load in enumerate(loads):
        if n != 1:
            load.wait()

    sst[...] = stack(DAMPING * smooth_ref[...])
    for i in range(mats.shape[2] // LANES):
        two = []
        for t in (2 * i, 2 * i + 1):
            two.append(coup_ref[t] if t < kinds_n else stiff_ref[...] if t == kinds_n else jnp.zeros((vals, vals), F32))
        both = jnp.concatenate(two, axis=1)
        mats[1, :, i * LANES:(i + 1) * LANES] = stack(both)
        mats[0, :, i * LANES:(i + 1) * LANES] = stack(times(sst[...], both))
    for i in range(rst.shape[1] // LANES):
        one, two = restr_ref[2 * i], restr_ref[2 * i + 1]
        cols = slice(i * LANES, (i + 1) * LANES)
        rst[:, cols] = stack(jnp.concatenate([one, two], axis=1))
        rtst[:, cols] = stack(jnp.concatenate([one.T, two.T], axis=1))
    pl.semaphore_wait(barrier, groups + curves - 2 + has_prev.astype(jnp.int32) + has_next.astype(jnp.int32))
    send_edges(0)

    rhs_e, rhs_i = edge_inner(rhs_ref)
    lev_e, lev_i = edge_inner(level_ref)
    scl_e, scl_i = jnp.exp2(lev_e.astype(F32)), jnp.exp2(lev_i.astype(F32))
    gs_e, gs_i = rhs_e * scl_e, rhs_i * scl_i
    nbr_e, nbr_i = edge_inner(nbr_ref)
    kind_e, kind_i = edge_inner(kind_ref)
    lane8 = lax.broadcasted_iota(jnp.int32, (8, LANES), 1)
    at_i = jnp.where(nbr_i != 0, lane8 + HALF + nbr_i, -1000)
    at_e = jnp.where(nbr_e != 0, jnp.where(lane8 < HALF, lane8, lane8 + LANES) + nbr_e, -1000)
    kind_e = jnp.where(nbr_e != 0, kind_e, -1)
    kind_i = jnp.where(nbr_i != 0, kind_i, -1)

    def couple(left, own, kinds, picks):
        slots_n = kinds.shape[0]
        picked = [picks(k) for k in range(slots_n)]
        codes, parts = [], []
        for k in range(slots_n):
            whole = picked[k]
            for other in range(k):
                same = kinds[other:other + 1] == kinds[k:k + 1]
                whole = whole + jnp.where(same, picked[other], 0.0)
            parts.append(stack(whole))
            codes.append(jnp.broadcast_to(kinds[k:k + 1].astype(F32), (2 * vals, LANES)).astype(BF16))
        empty = jnp.zeros_like(parts[0])

        def of_kind(t):
            if t >= kinds_n:
                return stack(own) if t == kinds_n else empty
            acc = empty
            for k in range(slots_n):
                acc = jnp.where(codes[k] == jnp.asarray(t, BF16), parts[k], acc)
            return acc

        totals = [None, None]
        chunk = 4
        for c in range(left.shape[1] // (chunk * vals)):
            found = [of_kind(t) for t in range(c * chunk, (c + 1) * chunk)]
            right = jnp.concatenate([
                jnp.concatenate([f[:vals] for f in found], axis=0),
                jnp.concatenate([f[vals:] for f in found], axis=0)], axis=1)
            r = jnp.dot(left[:, c * chunk * vals:(c + 1) * chunk * vals], right, preferred_element_type=F32)
            totals[c % 2] = r if totals[c % 2] is None else totals[c % 2] + r
        return fold(totals[0] + totals[1])

    def wide(row):
        return jnp.broadcast_to(row, (vals, LANES))

    def places(at):
        inner = (at >= HALF) & (at < HALF + LANES)
        own = (at >= 0) & (at < 2 * LANES)
        lane = at & (LANES - 1)
        return jnp.where(inner, lane ^ HALF, lane), jnp.where(inner, 1, jnp.where(own, 0, 2))

    lane_i, tile_i = places(at_i)
    lane_e, tile_e = places(at_e)

    def inner_image(left, e, i):
        def picks(k):
            lane = wide(lane_i[k:k + 1])
            return jnp.where(wide(tile_i[k:k + 1]) == 1, lane_take(i, lane), lane_take(e, lane))
        return couple(left, i, kind_i, picks)

    def edge_image(left, e, i, h):
        def picks(k):
            lane, tile = wide(lane_e[k:k + 1]), wide(tile_e[k:k + 1])
            got = jnp.where(tile == 0, lane_take(e, lane), lane_take(h, lane))
            return jnp.where(tile == 1, lane_take(i, lane), got)
        return couple(left, e, kind_e, picks)

    fix[0, 0], fix[0, 1] = times(sst[...], gs_e), times(sst[...], gs_i)
    fix[1, 0], fix[1, 1] = rhs_e, rhs_i
    fix[2, 0] = jnp.broadcast_to(1.0 / scl_e, (vals, LANES))
    fix[2, 1] = jnp.broadcast_to(1.0 / scl_i, (vals, LANES))
    cur[0], cur[1] = start_e, start_i

    lane_at = lane8
    own0_e, own0_i = edge_inner(own0_ref)
    at_one = jnp.where(lane_at < per_one, me_g * per_one + lane_at, 0)
    par1, oct1 = row_take(own1_ref, 0, at_one), row_take(own1_ref, 1, at_one)
    at_two = jnp.where(lane_at < own2_ref.shape[1], lane_at, 0)
    par2, oct2 = row_take(own2_ref, 0, at_two), row_take(own2_ref, 1, at_two)
    at_three = jnp.where(lane_at < per_three, me_c * per_three + lane_at, 0)
    par3, oct3 = row_take(own3_ref, 0, at_three), row_take(own3_ref, 1, at_three)

    slots_all, width = cnbr_ref.shape
    rep = LANES // width if width < LANES and LANES % width == 0 else 1
    rep = rep if slots_all % rep == 0 else 1
    rows_n = slots_all // rep
    cnb[...] = jnp.full_like(cnb, -1)
    ckd[...] = jnp.full_like(ckd, -1)
    clv[...] = jnp.zeros_like(clv)
    crow[...] = jnp.zeros_like(crow)
    for n in range(ctiles):
        size = min(LANES, width - n * LANES)
        cols = slice(n * LANES, n * LANES + size)
        for g in range(rep):
            rows, place = slice(g * rows_n, (g + 1) * rows_n), slice(g * size, (g + 1) * size)
            cnb[n, :rows_n, place] = cnbr_ref[rows, cols]
            ckd[n, :rows_n, place] = ckind_ref[rows, cols]
        clv[n, :, :size] = jnp.broadcast_to(clevel_ref[:, cols], (8, size))

    def to_group(off):
        return pltpu.make_async_remote_copy(
            src_ref=part, dst_ref=gpart.at[off], send_sem=gsend.at[off], recv_sem=grecv.at[off],
            device_id=(me_c, lax.rem(me_g + off, groups)), device_id_type=MESH)

    def to_curve(off):
        return pltpu.make_async_remote_copy(
            src_ref=hpart.at[me_c], dst_ref=hpart.at[me_c], send_sem=hsend.at[off], recv_sem=hrecv.at[off],
            device_id=(lax.rem(me_c + off, curves), me_g), device_id_type=MESH)

    def from_curve(off):
        who = lax.rem(me_c + curves - off, curves)
        return pltpu.make_async_remote_copy(
            src_ref=hpart.at[who], dst_ref=hpart.at[who], send_sem=hsend.at[off], recv_sem=hrecv.at[off],
            device_id=(lax.rem(me_c + off, curves), me_g), device_id_type=MESH)

    def middle():
        one = (gather_sum(octant_dot(rst[...], res[0], own0_e[1:2]), slots_of(own0_e[0:1]))
               + gather_sum(octant_dot(rst[...], res[1], own0_i[1:2]), slots_of(own0_i[0:1])))
        two = gather_sum(octant_dot(rst[...], one, oct1[0:1]), slots_of(par1[0:1]))
        three = gather_sum(octant_dot(rst[...], two, oct2[0:1]), slots_of(par2[0:1]))
        mapped = octant_dot(rst[...], three, oct3[0:1])
        ids = lax.broadcasted_iota(jnp.int32, (8, LANES), 0)
        slots = jnp.where(ids == par3[0:1], 1.0, 0.0).astype(BF16)
        hi, lo = split(mapped)
        zeros = jnp.zeros_like(hi)
        sums = (lax.dot_general(slots, jnp.concatenate([hi, zeros], axis=0), NT, preferred_element_type=F32)
                     + lax.dot_general(slots, jnp.concatenate([lo, zeros], axis=0), NT, preferred_element_type=F32))

        part[...] = sums[:per_four]
        over(groups, lambda off: to_group(off).start())
        over(groups, lambda off: to_group(off).wait_recv())
        mine = part[...]
        for off in range(1, groups):
            mine = mine + gpart[off]
        hpart[me_c] = mine
        over(curves, lambda off: to_curve(off).start())
        over(curves, lambda off: from_curve(off).wait_recv())

        for m in range(curves):
            crow[m * per_four:(m + 1) * per_four, :] = hpart[m]
        for n in range(ctiles):
            block = crow[n * LANES:(n + 1) * LANES, :].T[:vals]
            crhs[n] = times(sst[...], block * jnp.exp2(clv[n, 0:1].astype(F32)))
            cfield[0, n] = crhs[n]

        def coarse_step(s, carry):
            sweep, n = s // ctiles, lax.rem(s, ctiles)
            old = lax.rem(sweep, 2)
            at_c = cnb[n, :rows_n]
            kind_c = jnp.where(at_c >= 0, ckd[n, :rows_n], -1)
            field = [cfield[old, m] for m in range(ctiles)]
            own = cfield[old, n]

            def picks(k):
                at = wide(at_c[k:k + 1])
                lane = at & (LANES - 1)
                got = lane_take(field[0], lane)
                for m in range(1, ctiles):
                    got = jnp.where((at >> 7) == m, lane_take(field[m], lane), got)
                return got

            once = own
            if rep > 1:
                once = jnp.where(lax.broadcasted_iota(jnp.int32, own.shape, 1) < width, own, 0.0)
            image = couple(mats.at[0], once, kind_c, picks)
            total = image
            for g in range(1, rep):
                total = total + pltpu.roll(image, g * width, 1)
            cfield[1 - old, n] = own + (crhs[n] - total)
            return carry

        lax.fori_loop(0, (COARSE_SWEEPS - 1) * ctiles, coarse_step, 0)
        field = [cfield[(COARSE_SWEEPS - 1) % 2, m] for m in range(ctiles)]

        at = wide(jnp.where(lane_at < per_three, me_c * per_four + par3, 0)[0:1])
        back = lane_take(field[0], at & (LANES - 1))
        for s in range(1, ctiles):
            back = jnp.where((at >> 7) == s, lane_take(field[s], at & (LANES - 1)), back)
        back = octant_dot(rtst[...], back, oct3[0:1])
        back = octant_dot(rtst[...], lane_take(back, wide(par2[0:1])), oct2[0:1])
        back = octant_dot(rtst[...], lane_take(back, wide(par1[0:1])), oct1[0:1])
        e = cur[0] + octant_dot(rtst[...], lane_take(back, wide(own0_e[0:1])), own0_e[1:2])
        pack_edges(3, e)
        cur[0] = e
        send_edges(3)
        cur[1] = cur[1] + octant_dot(rtst[...], lane_take(back, wide(own0_i[0:1])), own0_i[1:2])

    def sweep(r, carry):
        @pl.when(r == 3)
        def _():
            middle()

        left = mats.at[(r == 2).astype(jnp.int32)]
        inner = inner_image(left, cur[0], cur[1])
        edge = edge_image(left, cur[0], cur[1], halo(r))

        @pl.when(r == 2)
        def _():
            res[0] = fix[1, 0] - edge * fix[2, 0]
            res[1] = fix[1, 1] - inner * fix[2, 1]

        @pl.when(r < 2)
        def _():
            new = cur[0] + (fix[0, 0] - edge)
            cur[0] = new
            cur[1] = cur[1] + (fix[0, 1] - inner)
            pack_edges(r + 1, new)
            send_edges(r + 1)

        @pl.when(r == 3)
        def _():
            low = lax.broadcasted_iota(jnp.int32, (vals, LANES), 1) < HALF
            for ref, e, i in ((base_ref, cur[0], cur[1]), (step_ref, fix[0, 0] - edge, fix[0, 1] - inner)):
                turned = swap(i)
                ref[:, :LANES] = jnp.where(low, e, turned)
                ref[:, LANES:] = jnp.where(low, turned, e)

        return carry

    lax.fori_loop(0, 4, sweep, 0)

    over(groups, lambda off: to_group(off).wait_send())
    over(curves, lambda off: to_curve(off).wait_send())

    @pl.when(has_prev)
    def _():
        for r in range(4):
            to_prev(r).wait_send()

    @pl.when(has_next)
    def _():
        for r in range(4):
            to_next(r).wait_send()


def solution(mesh):
    curves, groups = mesh.shape["curve"], mesh.shape["group"]

    def shards(*args):
        args = list(args)
        args[2] = args[2].reshape(1, -1)
        args[11] = args[11].reshape(1, -1)
        rhs, coup, restr = args[0], args[14], args[15]
        vals, blocks = rhs.shape
        kinds = coup.shape[0] + 1
        depth = -(-kinds // 4) * 4 * vals
        cw = -(-args[9].shape[1] // LANES) * LANES
        four = args[9].shape[1] // curves
        rdepth = restr.shape[0] * vals
        assert blocks == 2 * LANES and vals == HALF
        vm = pltpu.VMEM
        base, step = pl.pallas_call(
            functools.partial(kernel, curves, groups, len(args)),
            out_shape=[jax.ShapeDtypeStruct(rhs.shape, F32)] * 2,
            in_specs=[pl.BlockSpec(memory_space=pltpu.HBM)] * len(args),
            out_specs=[pl.BlockSpec(memory_space=pltpu.VMEM)] * 2,
            scratch_shapes=[vm(a.shape, a.dtype) for a in args] + [
                pltpu.SemaphoreType.DMA((len(args),)),
                vm((2, 2 * vals, depth), BF16),
                vm((2 * vals, rdepth), BF16),
                vm((2 * vals, rdepth), BF16),
                vm((2 * vals, vals), BF16),
                vm((cw // LANES, 8, LANES), jnp.int32),
                vm((cw // LANES, 8, LANES), jnp.int32),
                vm((cw // LANES, 8, LANES), jnp.int32),
                vm((2, cw // LANES, vals, LANES), F32),
                vm((cw // LANES, vals, LANES), F32),
                vm((cw, LANES), F32),
                vm((2, vals, LANES), F32),
                vm((2, vals, LANES), F32),
                vm((3, 2, vals, LANES), F32),
                vm((4, 2, vals // 2, LANES), F32),
                vm((4, vals // 2, LANES), F32),
                vm((4, vals // 2, LANES), F32),
                vm((four, LANES), F32),
                vm((groups, four, LANES), F32),
                vm((curves, four, LANES), F32),
                pltpu.SemaphoreType.DMA((4, 2)),
                pltpu.SemaphoreType.DMA((4, 2)),
                pltpu.SemaphoreType.DMA((groups,)),
                pltpu.SemaphoreType.DMA((groups,)),
                pltpu.SemaphoreType.DMA((curves,)),
                pltpu.SemaphoreType.DMA((curves,)),
            ],
            compiler_params=pltpu.CompilerParams(
                collective_id=0, has_side_effects=True, vmem_limit_bytes=60 * 2**20
            ),
        )(*args)
        return base + step

    fine, part, all_ = P(None, ("curve", "group")), P(None, "curve"), P()
    return jax.shard_map(
        shards,
        mesh=mesh,
        in_specs=(fine, fine, P(("curve", "group")), fine, fine, fine, part, part) + (all_,) * 8,
        out_specs=fine,
        check_vma=False,
    )
```
